32 devices in a mesh: rows: 8 (over y, x, core), depth: 4 (over z).
Axes of the slice: x: 2, y: 2, z: 4, core: 2. Of those that a mesh axis runs over, the one named last changes fastest.
Arguments:
- field: float32 [64, 64, 1024], P('rows', 'depth'), may hold values from 0 to 1
- diffusivity: bfloat16 [64, 64, 1024], P('rows', 'depth'), may hold values from 0.019897461 to 0.119628906
- velocity: bfloat16 [3, 64, 64, 1024], P(None, 'rows', 'depth'), may hold values from -1 to 1
Outputs:
- front: float32 [64, 64, 1024], P('rows', 'depth')
- picture: float32 [4, 64, 1024], P(None, 'rows', 'depth')
The draws below stay inside these ranges and needn't reach their ends.
All inputs are finite; a program needn't handle non-finite values.
Results may differ from the reference program's by a relative error of at most 0.0003.
Values sent between devices are 32-bit elements; how exact they have to be, the bound alone decides.
No kernel may reach another device: no remote copies, remote signals or barrier semaphores. Data moves between devices by JAX's collectives and lax.ppermute only.
A program may use at most 64 MiB of HBM per device.

```python
import math
import jax
import jax.numpy as jnp
from jax import lax

NY = 1024
NX = 64
NZ = 64


def block_scale(own_key, shape, split, smallest, top_value):
    def one(axis_at, shards_of):
        draws = jax.random.uniform(jax.random.fold_in(jax.random.fold_in(own_key, 6), axis_at), (shards_of,), jnp.float32, smallest / len(split), top_value / len(split))
        return jnp.repeat(jnp.exp(draws), shape[axis_at] // shards_of).reshape((-1,) + (1,) * (len(shape) - axis_at - 1))

    gain = one(*split[0])
    for cut in split[1:]:
        gain = gain * one(*cut)
    return gain


def setup_inputs(seed: int = 0) -> dict:
    arg_keys = jax.random.split(jax.random.key(seed), 4)
    field = jnp.clip(1.0 * jax.random.uniform(arg_keys[0], (NX, NZ, NY), jnp.float32) ** block_scale(arg_keys[0], (NX, NZ, NY), ((0, 8), (1, 4)), -0.2, 0.2), 0.0, 1.0)
    diffusivity = jnp.clip(jnp.exp(math.log(0.119628906) - 1.7938024 * jax.random.uniform(arg_keys[1], (NX, NZ, NY), jnp.float32) ** block_scale(arg_keys[1], (NX, NZ, NY), ((0, 8), (1, 4)), -0.2, 0.2)), 0.019897461, 0.119628906).astype(jnp.bfloat16)
    velocity = jnp.clip(jax.random.uniform(arg_keys[2], (3, NX, NZ, NY), jnp.float32, -1.0, 1.0) * block_scale(arg_keys[2], (3, NX, NZ, NY), ((1, 8), (2, 4)), -0.4, 0.0), -1.0, 1.0).astype(jnp.bfloat16)
    return {"field": field, "diffusivity": diffusivity, "velocity": velocity}


time_step = 0.2
growth_rate = 1.0
opacity_total = 3.0


def upwind(speed, center, behind, ahead):
    return jnp.maximum(speed, 0.0) * (center - behind) + jnp.minimum(speed, 0.0) * (ahead - center)


def evolve(extended, diffusivity, velocity):
    padded = jnp.pad(extended, ((0, 0), (0, 0), (1, 1)))
    center = padded[1:-1, 1:-1, 1:-1]
    row_after = padded[2:, 1:-1, 1:-1]
    row_before = padded[:-2, 1:-1, 1:-1]
    deep_after = padded[1:-1, 2:, 1:-1]
    deep_before = padded[1:-1, :-2, 1:-1]
    col_after = padded[1:-1, 1:-1, 2:]
    col_before = padded[1:-1, 1:-1, :-2]
    laplace = row_after + row_before + deep_after + deep_before + col_after + col_before - 6.0 * center
    transport = upwind(velocity[0], center, row_before, row_after)
    transport = transport + upwind(velocity[1], center, deep_before, deep_after)
    transport = transport + upwind(velocity[2], center, col_before, col_after)
    return center + time_step * (diffusivity * laplace - transport + growth_rate * center * (1.0 - center))


def render(extended, opacity):
    padded = jnp.pad(extended, ((0, 0), (0, 0), (1, 1)))
    center = padded[1:-1, 1:-1, 1:-1]
    grad_row = (padded[2:, 1:-1, 1:-1] - padded[:-2, 1:-1, 1:-1]) * 0.5
    grad_deep = (padded[1:-1, 2:, 1:-1] - padded[1:-1, :-2, 1:-1]) * 0.5
    grad_col = (padded[1:-1, 1:-1, 2:] - padded[1:-1, 1:-1, :-2]) * 0.5
    lighting = 0.48 * grad_row + 0.64 * grad_deep + 0.6 * grad_col
    magnitude = grad_row * grad_row + grad_deep * grad_deep + grad_col * grad_col + 0.1
    shade = 0.35 + 0.65 * lighting * lighting / magnitude
    optical = opacity * center
    through = jnp.cumsum(optical, axis=1)
    weight = jnp.exp(optical - through) * (1.0 - jnp.exp(-optical)) * shade
    red = jnp.sum(weight * center, axis=1)
    green = jnp.sum(weight * center * center, axis=1)
    blue = jnp.sum(weight * (1.0 - center), axis=1)
    remain = jnp.exp(-through[:, -1])
    return jnp.stack([red, green, blue, remain])


def ref_section(field, diffusivity, velocity):
    padded = jnp.pad(field, ((1, 1), (1, 1), (0, 0)))
    row_block = math.gcd(NX, 8)

    def advance(block_index):
        first_row = block_index * row_block
        extended = lax.dynamic_slice_in_dim(padded, first_row, row_block + 2, 0)
        local_diff = lax.dynamic_slice_in_dim(diffusivity, first_row, row_block, 0).astype(jnp.float32)
        local_vel = lax.dynamic_slice_in_dim(velocity, first_row, row_block, 1).astype(jnp.float32)
        return evolve(extended, local_diff, local_vel)

    pieces = lax.map(advance, jnp.arange(NX // row_block, dtype=jnp.int32))
    return pieces.reshape(NX, NZ, NY)


def ref_render(front):
    padded = jnp.pad(front, ((1, 1), (1, 1), (0, 0)))
    row_block = math.gcd(NX, 8)

    def shine(block_index):
        first_row = block_index * row_block
        extended = lax.dynamic_slice_in_dim(padded, first_row, row_block + 2, 0)
        return render(extended, opacity_total / NZ)

    pieces = lax.map(shine, jnp.arange(NX // row_block, dtype=jnp.int32))
    return pieces.transpose(1, 0, 2, 3).reshape(4, NX, NY)


def reference(field, diffusivity, velocity):
    middle = ref_section(field, diffusivity, velocity)
    front = ref_section(middle, diffusivity, velocity)
    picture = ref_render(front)
    return front, picture
```

```python
import jax
import jax.numpy as jnp
from jax import lax
from jax.experimental import pallas as pl
from jax.experimental.pallas import tpu as pltpu
from jax.sharding import PartitionSpec as P

time_step = 0.2
growth_rate = 1.0
opacity_total = 3.0

lanes = 128
margin = 8


def pairs(count, first):
    forward = [(i, i + 1) for i in range(first, count - 1, 2)]
    return forward + [(target, source) for source, target in forward]


def swap_pairs(value, axis, first):
    return lax.ppermute(value, axis, pairs(lax.axis_size(axis), first))


def stencil(u, low, high, coef):
    diff = coef[0]
    change = growth_rate * u * (1.0 - u)
    for before, after, speed in zip(low, high, coef[1:]):
        change = change + (diff + jnp.maximum(speed, 0.0)) * (before - u)
        change = change + (diff - jnp.minimum(speed, 0.0)) * (after - u)
    return u + time_step * change


def beside(chunks):
    lane = lax.broadcasted_iota(jnp.int32, chunks[0].shape, 1)
    right = [pltpu.roll(x, 1, 1) for x in chunks]
    left = [pltpu.roll(x, lanes - 1, 1) for x in chunks]
    zero = jnp.zeros_like(chunks[0])
    count = len(chunks)
    before = [jnp.where(lane == 0, right[c - 1] if c else zero, right[c]) for c in range(count)]
    after = [
        jnp.where(lane == lanes - 1, left[c + 1] if c + 1 < count else zero, left[c])
        for c in range(count)
    ]
    return before, after


def cols(c):
    return slice(c * lanes, (c + 1) * lanes)


def pack_kernel(field, diff, vel, even_d, odd_d, even_r, odd_r, flat, coefs):
    rows, depth, width = field.shape
    count = width // lanes
    depth_odd = lax.axis_index("depth") % 2 == 1
    rows_odd = lax.axis_index("rows") % 2 == 1

    def coef_row(r, c):
        return [diff[r, :, cols(c)].astype(jnp.float32)] + [
            vel[i, r, :, cols(c)].astype(jnp.float32) for i in range(3)
        ]

    for c in range(count):
        for r in range(rows):
            place = pl.ds(r * depth, depth)
            flat[c, place, :] = field[r, :, cols(c)]
            for i, value in enumerate(coef_row(r, c)):
                coefs[i, c, place, :] = value
        first = [field[0, :, cols(c)], field[1, :, cols(c)]] + coef_row(0, c)
        last = [field[rows - 1, :, cols(c)], field[rows - 2, :, cols(c)]] + coef_row(rows - 1, c)
        for i in range(6):
            even_r[i, :, cols(c)] = jnp.where(rows_odd, first[i], last[i])
            odd_r[i, :, cols(c)] = jnp.where(rows_odd, last[i], first[i])

    row = lax.broadcasted_iota(jnp.int32, (rows, lanes), 0)
    sides = []
    for near, step in ((0, 1), (depth - 1, -1)):

        def slab(ref, d):
            return [ref[c, pl.ds(d, rows, stride=depth), :] for c in range(count)]

        u0, u1, u2 = (slab(flat, near + step * j) for j in range(3))
        near_coef = [slab(coefs.at[i], near) for i in range(4)]
        next_coef = [slab(coefs.at[i], near + step) for i in range(4)]
        before, after = beside(u1)
        side = []
        for c in range(count):
            above = jnp.where(row == 0, 0.0, pltpu.roll(u1[c], 1, 0))
            below = jnp.where(row == rows - 1, 0.0, pltpu.roll(u1[c], rows - 1, 0))
            deep = (u0[c], u2[c]) if step > 0 else (u2[c], u0[c])
            coef = [next_coef[i][c] for i in range(4)]
            middle = stencil(
                u1[c], (above, deep[0], before[c]), (below, deep[1], after[c]), coef
            )
            outer = jnp.where(row == 0, jnp.maximum(coef[1], 0.0), -jnp.minimum(coef[1], 0.0))
            weight = time_step * (coef[0] + outer)
            side.append([u0[c], u1[c]] + [near_coef[i][c] for i in range(4)] + [middle, weight])
        sides.append(side)
    low, high = sides
    for c in range(count):
        for i in range(8):
            even_d[i, :, cols(c)] = jnp.where(depth_odd, low[c][i], high[c][i])
            odd_d[i, :, cols(c)] = jnp.where(depth_odd, high[c][i], low[c][i])


def arrived(even, odd, is_odd, index):
    a, b = even[index], odd[index]
    return jnp.where(is_odd, a, b), jnp.where(is_odd, b, a)


def corner_kernel(field, diff, vel, even_d, odd_d, even_2, odd_2, ext):
    rows, depth, width = field.shape
    count = width // lanes
    depth_odd = lax.axis_index("depth") % 2 == 1
    rows_odd = lax.axis_index("rows") % 2 == 1
    sides = []
    for edge, inner in ((0, 1), (rows - 1, rows - 2)):
        far = 2 * inner - edge
        u = [field[inner, :, cols(c)] for c in range(count)]
        before, after = beside(u)
        side = []
        for c in range(count):
            low, high = arrived(even_d, odd_d, depth_odd, (0, pl.ds(inner, 1), cols(c)))
            ext[c, margin - 1 : margin, :] = low
            ext[c, margin : margin + depth, :] = u[c]
            ext[c, margin + depth : margin + depth + 1, :] = high
            shallow = ext[c, pl.ds(margin - 1, depth), :]
            deep = ext[c, pl.ds(margin + 1, depth), :]
            outer, further = field[edge, :, cols(c)], field[far, :, cols(c)]
            above, below = (outer, further) if edge < inner else (further, outer)
            coef = [diff[inner, :, cols(c)].astype(jnp.float32)] + [
                vel[i, inner, :, cols(c)].astype(jnp.float32) for i in range(3)
            ]
            side.append(stencil(u[c], (above, shallow, before[c]), (below, deep, after[c]), coef))
        sides.append(side)
    first, last = sides
    for c in range(count):
        even_2[:depth, cols(c)] = jnp.where(rows_odd, first[c], last[c])
        odd_2[:depth, cols(c)] = jnp.where(rows_odd, last[c], first[c])
    for j, (item, second) in enumerate(
        ((0, False), (1, False), (0, True), (2, False), (3, False), (4, False), (5, False))
    ):
        at_first = 1 if second else 0
        at_last = rows - 1 - at_first
        for c in range(count):
            f_low, f_high = arrived(even_d, odd_d, depth_odd, (item, pl.ds(at_first, 1), cols(c)))
            l_low, l_high = arrived(even_d, odd_d, depth_odd, (item, pl.ds(at_last, 1), cols(c)))
            for k, f_val, l_val in ((0, f_low, l_low), (1, f_high, l_high)):
                place = depth + 8 * k + j
                even_2[place : place + 1, cols(c)] = jnp.where(rows_odd, f_val, l_val)
                odd_2[place : place + 1, cols(c)] = jnp.where(rows_odd, l_val, f_val)


def main_kernel(
    opacity, field, diff, vel, even_d, odd_d, even_r, odd_r, even_2, odd_2,
    front, partial, first, second, third, slabs,
):
    rows, depth, width = field.shape
    count = width // lanes
    pitch = depth + 2 * margin
    depth_odd = lax.axis_index("depth") % 2 == 1
    rows_odd = lax.axis_index("rows") % 2 == 1
    every = range(count)

    def at(r, d):
        return (r + 2) * pitch + margin + d

    def line(ref, r, d=0):
        return [ref[c, pl.ds(at(r, d), depth), :] for c in every]

    def slab(ref, r, d, length):
        return [ref[c, pl.ds(at(r, d), length, stride=pitch), :] for c in every]

    for c in every:
        for r in range(rows):
            first[c, pl.ds(at(r, 0), depth), :] = field[r, :, cols(c)]
        for j in range(2):
            low, high = arrived(even_r, odd_r, rows_odd, (j, slice(None), cols(c)))
            first[c, pl.ds(at(-1 - j, 0), depth), :] = low
            first[c, pl.ds(at(rows + j, 0), depth), :] = high
            low, high = arrived(even_d, odd_d, depth_odd, (j, slice(None), cols(c)))
            first[c, pl.ds(at(0, -1 - j), rows, stride=pitch), :] = low
            first[c, pl.ds(at(0, depth + j), rows, stride=pitch), :] = high
        for j, r, d in ((0, 1, 1), (1, 1, 2), (2, 2, 1)):
            for k, deep in ((0, -d), (1, depth - 1 + d)):
                place = depth + 8 * k + j
                low, high = arrived(even_2, odd_2, rows_odd, (slice(place, place + 1), cols(c)))
                first[c, pl.ds(at(-r, deep), 1), :] = low
                first[c, pl.ds(at(rows - 1 + r, deep), 1), :] = high
        for i in range(4):
            both = arrived(even_d, odd_d, depth_odd, (2 + i, slice(None), cols(c)))
            for k in range(2):
                slabs[k, i, c, 1 : rows + 1, :] = both[k]
                place = depth + 8 * k + 3 + i
                low, high = arrived(even_2, odd_2, rows_odd, (slice(place, place + 1), cols(c)))
                slabs[k, i, c, 0:1, :] = low
                slabs[k, i, c, rows + 1 : rows + 2, :] = high
        low, high = arrived(even_2, odd_2, rows_odd, (slice(0, depth), cols(c)))
        second[c, pl.ds(at(-2, 0), depth), :] = low
        second[c, pl.ds(at(rows + 1, 0), depth), :] = high

    row = lax.broadcasted_iota(jnp.int32, (rows, lanes), 0)
    for k, d in ((0, -2), (1, depth + 1)):
        above, below = slab(first, -1, d, rows), slab(first, 1, d, rows)
        for c in every:
            partly = arrived(even_d, odd_d, depth_odd, (6, slice(None), cols(c)))[k]
            weight = arrived(even_d, odd_d, depth_odd, (7, slice(None), cols(c)))[k]
            extra = jnp.where(row == 0, above[c], jnp.where(row == rows - 1, below[c], 0.0))
            second[c, pl.ds(at(0, d), rows, stride=pitch), :] = partly + weight * extra

    def section_line(source, r, coef):
        u = line(source, r)
        before, after = beside(u)
        low = (line(source, r - 1), line(source, r, -1), before)
        high = (line(source, r + 1), line(source, r, 1), after)
        return [
            stencil(u[c], [x[c] for x in low], [x[c] for x in high], coef(c)) for c in every
        ]

    def section_slab(source, r, d, length, coef):
        u = slab(source, r, d, length)
        before, after = beside(u)
        low = (slab(source, r - 1, d, length), slab(source, r, d - 1, length), before)
        high = (slab(source, r + 1, d, length), slab(source, r, d + 1, length), after)
        return [
            stencil(u[c], [x[c] for x in low], [x[c] for x in high], coef(c)) for c in every
        ]

    def own_coef(r):
        return lambda c: [diff[r, :, cols(c)].astype(jnp.float32)] + [
            vel[i, r, :, cols(c)].astype(jnp.float32) for i in range(3)
        ]

    def beyond_coef(k):
        return lambda c: [
            arrived(even_r, odd_r, rows_odd, (2 + i, slice(None), cols(c)))[k] for i in range(4)
        ]

    def slab_coef(k, start, length):
        return lambda c: [slabs[k, i, c, start : start + length, :] for i in range(4)]

    def own_middle(r, carry):
        for c, value in enumerate(section_line(first, r, own_coef(r))):
            second[c, pl.ds(at(r, 0), depth), :] = value
        return carry

    lax.fori_loop(0, rows, own_middle, 0)
    for k, r in ((0, -1), (1, rows)):
        for c, value in enumerate(section_line(first, r, beyond_coef(k))):
            second[c, pl.ds(at(r, 0), depth), :] = value
    for k, d in ((0, -1), (1, depth)):
        values = section_slab(first, -1, d, rows + 2, slab_coef(k, 0, rows + 2))
        for c, value in enumerate(values):
            second[c, pl.ds(at(-1, d), rows + 2, stride=pitch), :] = value

    def own_front(r, carry):
        for c, value in enumerate(section_line(second, r, own_coef(r))):
            third[c, pl.ds(at(r, 0), depth), :] = value
            front[r, :, cols(c)] = value
        return carry

    lax.fori_loop(0, rows, own_front, 0)
    for k, r in ((0, -1), (1, rows)):
        for c, value in enumerate(section_line(second, r, beyond_coef(k))):
            third[c, pl.ds(at(r, 0), depth), :] = value
    for k, d in ((0, -1), (1, depth)):
        values = section_slab(second, 0, d, rows, slab_coef(k, 1, rows))
        for c, value in enumerate(values):
            third[c, pl.ds(at(0, d), rows, stride=pitch), :] = value

    def shine(d, carry):
        center = slab(third, 0, d, rows)
        before, after = beside(center)
        above, below = slab(third, -1, d, rows), slab(third, 1, d, rows)
        shallow, deep = slab(third, 0, d - 1, rows), slab(third, 0, d + 1, rows)
        result = []
        for c in every:
            through, total, red, green = carry[c]
            u = center[c]
            grad_row = below[c] - above[c]
            grad_deep = deep[c] - shallow[c]
            grad_col = after[c] - before[c]
            lighting = 0.48 * grad_row + 0.64 * grad_deep + 0.6 * grad_col
            magnitude = grad_row * grad_row + grad_deep * grad_deep + grad_col * grad_col + 0.4
            shade = 0.35 + 0.65 * lighting * lighting / magnitude
            passed = jnp.exp(-opacity * u)
            weight = through * (1.0 - passed) * shade
            colored = weight * u
            result.append((through * passed, total + weight, red + colored, green + colored * u))
        return tuple(result)

    zero, one = jnp.zeros((rows, lanes), jnp.float32), jnp.ones((rows, lanes), jnp.float32)
    carry = tuple((one, zero, zero, zero) for _ in every)
    for d in range(depth):
        carry = shine(d, carry)
    for c, (through, total, red, green) in enumerate(carry):
        partial[0, :, cols(c)] = red
        partial[1, :, cols(c)] = green
        partial[2, :, cols(c)] = total - red
        partial[3, :, cols(c)] = through


def vmem(shape):
    return pltpu.VMEM(shape, jnp.float32)


def here(value):
    return pltpu.with_memory_space_constraint(value, pltpu.VMEM)


def shards(field, diffusivity, velocity):
    rows, depth, width = field.shape
    count = width // lanes
    pitch = depth + 2 * margin
    groups = lax.axis_size("depth")
    params = pltpu.CompilerParams(vmem_limit_bytes=24 * 2**20)

    even_d, odd_d, even_r, odd_r = pl.pallas_call(
        pack_kernel,
        out_shape=[vmem((8, rows, width))] * 2 + [vmem((6, depth, width))] * 2,
        scratch_shapes=[
            pltpu.VMEM((count, rows * depth, lanes), jnp.float32),
            pltpu.VMEM((4, count, rows * depth, lanes), jnp.float32),
        ],
        compiler_params=params,
        name="pack",
    )(field, diffusivity, velocity)
    even_d = here(swap_pairs(even_d, "depth", 0))
    odd_d = here(swap_pairs(odd_d, "depth", 1))
    even_r = here(swap_pairs(even_r, "rows", 0))
    odd_r = here(swap_pairs(odd_r, "rows", 1))
    own = (here(field), here(diffusivity), here(velocity))
    even_2, odd_2 = pl.pallas_call(
        corner_kernel,
        out_shape=[vmem((depth + 16, width))] * 2,
        scratch_shapes=[pltpu.VMEM((count, pitch, lanes), jnp.float32)],
        compiler_params=params,
        name="corner",
    )(*own, even_d, odd_d)
    even_2 = here(swap_pairs(even_2, "rows", 0))
    odd_2 = here(swap_pairs(odd_2, "rows", 1))
    opacity = opacity_total / (depth * groups)
    front, partial = pl.pallas_call(
        lambda *refs: main_kernel(opacity, *refs),
        out_shape=[jax.ShapeDtypeStruct(field.shape, jnp.float32), vmem((4, rows, width))],
        scratch_shapes=[pltpu.VMEM((count, (rows + 4) * pitch, lanes), jnp.float32)] * 3
        + [pltpu.VMEM((2, 4, count, rows + 8, lanes), jnp.float32)],
        compiler_params=params,
        name="main",
    )(*own, even_d, odd_d, even_r, odd_r, even_2, odd_2)

    position = lax.axis_index("depth")
    split = partial.reshape(4, rows, groups, width // groups)
    parts = []
    for apart in range(groups):
        part = lax.dynamic_index_in_dim(split, position ^ apart, 2, keepdims=False)
        if apart:
            part = lax.ppermute(part, "depth", [(i, i ^ apart) for i in range(groups)])
        parts.append(part)
    parts = jnp.stack(parts)
    picture = None
    for s in range(groups):
        segment = lax.dynamic_index_in_dim(parts, position ^ s, 0, keepdims=False)
        if picture is None:
            colors, through = segment[:3], segment[3:]
            picture = (colors, through)
        else:
            colors = colors + through * segment[:3]
            through = through * segment[3:]
    return front, jnp.concatenate([colors, through], axis=0)


def solution(mesh):
    return jax.shard_map(
        shards,
        mesh=mesh,
        in_specs=(
            P("rows", "depth", None),
            P("rows", "depth", None),
            P(None, "rows", "depth", None),
        ),
        out_specs=(P("rows", "depth", None), P(None, "rows", "depth")),
        check_vma=False,
    )
```

```python
import jax
import jax.numpy as jnp
from jax import lax
from jax.experimental import pallas as pl
from jax.experimental.pallas import tpu as pltpu
from jax.sharding import PartitionSpec as P

time_step = 0.2
growth_rate = 1.0
opacity_total = 3.0

lanes = 128
margin = 8


def pairs(count, first):
    forward = [(i, i + 1) for i in range(first, count - 1, 2)]
    return forward + [(target, source) for source, target in forward]


def swap_pairs(value, axis, first):
    return lax.ppermute(value, axis, pairs(lax.axis_size(axis), first))


def stencil(u, low, high, coef):
    diff = coef[0]
    change = growth_rate * u * (1.0 - u)
    for before, after, speed in zip(low, high, coef[1:]):
        change = change + (diff + jnp.maximum(speed, 0.0)) * (before - u)
        change = change + (diff - jnp.minimum(speed, 0.0)) * (after - u)
    return u + time_step * change


def beside(chunks):
    lane = lax.broadcasted_iota(jnp.int32, chunks[0].shape, 1)
    right = [pltpu.roll(x, 1, 1) for x in chunks]
    left = [pltpu.roll(x, lanes - 1, 1) for x in chunks]
    zero = jnp.zeros_like(chunks[0])
    count = len(chunks)
    before = [jnp.where(lane == 0, right[c - 1] if c else zero, right[c]) for c in range(count)]
    after = [
        jnp.where(lane == lanes - 1, left[c + 1] if c + 1 < count else zero, left[c])
        for c in range(count)
    ]
    return before, after


def cols(c):
    return slice(c * lanes, (c + 1) * lanes)


def coef_of(diff, vel, r, c):
    return [diff[r, :, cols(c)].astype(jnp.float32)] + [
        vel[i, r, :, cols(c)].astype(jnp.float32) for i in range(3)
    ]


def weight_low(diff, speed):
    return time_step * (diff + jnp.maximum(speed, 0.0))


def weight_high(diff, speed):
    return time_step * (diff - jnp.minimum(speed, 0.0))


def pack_kernel(
    field_far, diff_far, vel_far, field, diff, vel, even_d, odd_d, even_r, odd_r, flat, coefs, sems
):
    loads = [
        pltpu.make_async_copy(source, target, sems.at[i])
        for i, (source, target) in enumerate(
            ((field_far, field), (diff_far, diff), (vel_far, vel))
        )
    ]
    for load in loads:
        load.start()
    for load in loads:
        load.wait()
    rows, depth, width = field.shape
    count = width // lanes
    depth_odd = lax.axis_index("depth") % 2 == 1
    rows_odd = lax.axis_index("rows") % 2 == 1

    for c in range(count):
        for r in range(rows):
            place = pl.ds(r * depth, depth)
            coef = coef_of(diff, vel, r, c)
            flat[c, place, :] = field[r, :, cols(c)]
            for i in range(4):
                coefs[i, c, place, :] = coef[i]
            if r == 0:
                first = (field[r, :, cols(c)], weight_low(coef[0], coef[1]))
            if r == rows - 1:
                last = (field[r, :, cols(c)], weight_high(coef[0], coef[1]))
        for i in range(2):
            even_r[i, :, cols(c)] = jnp.where(rows_odd, first[i], last[i])
            odd_r[i, :, cols(c)] = jnp.where(rows_odd, last[i], first[i])

    row = lax.broadcasted_iota(jnp.int32, (rows, lanes), 0)
    sides = []
    for near, step in ((0, 1), (depth - 1, -1)):

        def slab(ref, d):
            return [ref[c, pl.ds(d, rows, stride=depth), :] for c in range(count)]

        u0, u1, u2 = (slab(flat, near + step * j) for j in range(3))
        near_coef = [slab(coefs.at[i], near) for i in range(4)]
        next_coef = [slab(coefs.at[i], near + step) for i in range(4)]
        before, after = beside(u1)
        side = []
        for c in range(count):
            above = jnp.where(row == 0, 0.0, pltpu.roll(u1[c], 1, 0))
            below = jnp.where(row == rows - 1, 0.0, pltpu.roll(u1[c], rows - 1, 0))
            deep = (u0[c], u2[c]) if step > 0 else (u2[c], u0[c])
            coef = [next_coef[i][c] for i in range(4)]
            middle = stencil(
                u1[c], (above, deep[0], before[c]), (below, deep[1], after[c]), coef
            )
            weight = jnp.where(
                row == 0, weight_low(coef[0], coef[1]), weight_high(coef[0], coef[1])
            )
            side.append([u0[c], u1[c]] + [near_coef[i][c] for i in range(4)] + [middle, weight])
        sides.append(side)
    low, high = sides
    for c in range(count):
        for i in range(8):
            even_d[i, :, cols(c)] = jnp.where(depth_odd, low[c][i], high[c][i])
            odd_d[i, :, cols(c)] = jnp.where(depth_odd, high[c][i], low[c][i])


def arrived(even, odd, is_odd, index):
    a, b = even[index], odd[index]
    return jnp.where(is_odd, a, b), jnp.where(is_odd, b, a)


def edge_kernel(
    field, diff, vel, even_d, odd_d, even_r, odd_r, even_2, odd_2, middles, ext, edge
):
    rows, depth, width = field.shape
    every = range(width // lanes)
    depth_odd = lax.axis_index("depth") % 2 == 1
    rows_odd = lax.axis_index("rows") % 2 == 1
    own = pl.ds(margin, depth)
    shallow, deep = pl.ds(margin - 1, depth), pl.ds(margin + 1, depth)
    beyond = [arrived(even_r, odd_r, rows_odd, (0, slice(None), cols(c))) for c in every]
    lines = (0, 1, rows - 2, rows - 1)
    values = {r: [field[r, :, cols(c)] for c in every] for r in lines + (2, rows - 3)}
    values[-1] = [x[0] for x in beyond]
    values[rows] = [x[1] for x in beyond]
    coefs = {r: [coef_of(diff, vel, r, c) for c in every] for r in lines}
    for j, r in enumerate(lines):
        u = values[r]
        before, after = beside(u)
        for c in every:
            low, high = arrived(even_d, odd_d, depth_odd, (0, pl.ds(r, 1), cols(c)))
            ext[j, c, margin - 1 : margin, :] = low
            ext[j, c, own, :] = u[c]
            ext[j, c, margin + depth : margin + depth + 1, :] = high
        for c in every:
            middles[j, :, cols(c)] = stencil(
                u[c],
                (values[r - 1][c], ext[j, c, shallow, :], before[c]),
                (values[r + 1][c], ext[j, c, deep, :], after[c]),
                coefs[r][c],
            )
    zero = jnp.zeros((1, lanes), jnp.float32)
    none = jnp.zeros((depth, lanes), jnp.float32)
    sides = []
    for j, inner, r in ((0, 1, 0), (3, 2, rows - 1)):
        u = [middles[j, :, cols(c)] for c in every]
        before, after = beside(u)
        side = []
        for c in every:
            edge[j // 3, c, margin - 1 : margin, :] = zero
            edge[j // 3, c, own, :] = u[c]
            edge[j // 3, c, margin + depth : margin + depth + 1, :] = zero
        for c in every:
            next_row = middles[inner, :, cols(c)]
            above, below = (none, next_row) if r == 0 else (next_row, none)
            coef = coefs[r][c]
            partly = stencil(
                u[c],
                (above, edge[j // 3, c, shallow, :], before[c]),
                (below, edge[j // 3, c, deep, :], after[c]),
                coef,
            )
            side.append(
                (u[c], partly, weight_low(coef[0], coef[2]), weight_high(coef[0], coef[2]))
            )
        sides.append(side)
    first, last = sides
    for c in every:
        for i in range(2):
            place = pl.ds(i * depth, depth)
            even_2[place, cols(c)] = jnp.where(rows_odd, first[c][i], last[c][i])
            odd_2[place, cols(c)] = jnp.where(rows_odd, last[c][i], first[c][i])
        for k, d in ((0, 0), (1, depth - 1)):
            place = 2 * depth + 8 * k + 7
            f_val, l_val = first[c][2 + k][d : d + 1], last[c][2 + k][d : d + 1]
            even_2[place : place + 1, cols(c)] = jnp.where(rows_odd, f_val, l_val)
            odd_2[place : place + 1, cols(c)] = jnp.where(rows_odd, l_val, f_val)
    for j, (item, f_row) in enumerate(
        ((0, 0), (1, 0), (0, 1), (2, 0), (3, 0), (4, 0), (5, 0))
    ):
        l_row = rows - 1 - f_row
        for c in every:
            f_both = arrived(even_d, odd_d, depth_odd, (item, pl.ds(f_row, 1), cols(c)))
            l_both = arrived(even_d, odd_d, depth_odd, (item, pl.ds(l_row, 1), cols(c)))
            for k in range(2):
                place = 2 * depth + 8 * k + j
                even_2[place : place + 1, cols(c)] = jnp.where(rows_odd, f_both[k], l_both[k])
                odd_2[place : place + 1, cols(c)] = jnp.where(rows_odd, l_both[k], f_both[k])


class Block:
    def __init__(self, rows, depth, width):
        self.rows, self.depth, self.every = rows, depth, range(width // lanes)
        self.pitch = depth + 2 * margin

    def at(self, r, d):
        return (r + 2) * self.pitch + margin + d

    def along(self, r, d=0):
        return pl.ds(self.at(r, d), self.depth)

    def across(self, r, d, length):
        return pl.ds(self.at(r, d), length, stride=self.pitch)

    def line(self, ref, r, d=0):
        return [ref[c, self.along(r, d), :] for c in self.every]

    def slab(self, ref, r, d, length):
        return [ref[c, self.across(r, d, length), :] for c in self.every]

    def put(self, ref, place, values):
        for c in self.every:
            ref[c, place, :] = values[c]

    def section_line(self, ref, r, coef):
        u = self.line(ref, r)
        before, after = beside(u)
        low = (self.line(ref, r - 1), self.line(ref, r, -1), before)
        high = (self.line(ref, r + 1), self.line(ref, r, 1), after)
        return [
            stencil(u[c], [x[c] for x in low], [x[c] for x in high], coef(c)) for c in self.every
        ]

    def section_slab(self, ref, r, d, length, coef):
        u = self.slab(ref, r, d, length)
        before, after = beside(u)
        low = (self.slab(ref, r - 1, d, length), self.slab(ref, r, d - 1, length), before)
        high = (self.slab(ref, r + 1, d, length), self.slab(ref, r, d + 1, length), after)
        return [
            stencil(u[c], [x[c] for x in low], [x[c] for x in high], coef(c)) for c in self.every
        ]


def inner_kernel(
    field, diff, vel, even_d, odd_d, even_r, odd_r, middles, first, second, third, slabs, front
):
    rows, depth, width = field.shape
    block = Block(rows, depth, width)
    depth_odd = lax.axis_index("depth") % 2 == 1
    rows_odd = lax.axis_index("rows") % 2 == 1
    for c in block.every:
        for r in range(rows):
            first[c, block.along(r), :] = field[r, :, cols(c)]
        low, high = arrived(even_r, odd_r, rows_odd, (0, slice(None), cols(c)))
        first[c, block.along(-1), :] = low
        first[c, block.along(rows), :] = high
        for j in range(2):
            low, high = arrived(even_d, odd_d, depth_odd, (j, slice(None), cols(c)))
            first[c, block.across(0, -1 - j, rows), :] = low
            first[c, block.across(0, depth + j, rows), :] = high
        for i in range(4):
            both = arrived(even_d, odd_d, depth_odd, (2 + i, slice(None), cols(c)))
            for k in range(2):
                slabs[k, i, c, 1 : rows + 1, :] = both[k]
        for j, r in enumerate((0, 1, rows - 2, rows - 1)):
            second[c, block.along(r), :] = middles[j, :, cols(c)]

    def own_middle(r, carry):
        values = block.section_line(first, r, lambda c: coef_of(diff, vel, r, c))
        block.put(second, block.along(r), values)
        return carry

    lax.fori_loop(2, rows - 2, own_middle, 0)
    for k, d in ((0, -1), (1, depth)):
        values = block.section_slab(
            first, 1, d, rows - 2, lambda c: [slabs[k, i, c, 2:rows, :] for i in range(4)]
        )
        block.put(second, block.across(1, d, rows - 2), values)

    def own_front(r, carry):
        values = block.section_line(second, r, lambda c: coef_of(diff, vel, r, c))
        block.put(third, block.along(r), values)
        for c in block.every:
            front[r, :, cols(c)] = values[c]
        return carry

    lax.fori_loop(1, rows - 1, own_front, 0)


def rim_kernel(
    opacity, diff, vel, even_d, odd_d, even_r, odd_r, even_2, odd_2, *refs
):
    first, second, third, slabs, front, front_far, partial, sem = refs[5:]
    rows, depth, width = front.shape
    block = Block(rows, depth, width)
    every = block.every
    depth_odd = lax.axis_index("depth") % 2 == 1
    rows_odd = lax.axis_index("rows") % 2 == 1
    row = lax.broadcasted_iota(jnp.int32, (rows, lanes), 0)

    def corner(k, j, c):
        place = 2 * depth + 8 * k + j
        return arrived(even_2, odd_2, rows_odd, (slice(place, place + 1), cols(c)))

    for c in every:
        for k, step in ((0, -1), (1, 1)):
            near = -1 if k == 0 else depth
            for j, r, d in ((0, 1, near), (1, 1, near + step), (2, 2, near)):
                low, high = corner(k, j, c)
                first[c, pl.ds(block.at(-r, d), 1), :] = low
                first[c, pl.ds(block.at(rows - 1 + r, d), 1), :] = high
            for i in range(4):
                low, high = corner(k, 3 + i, c)
                slabs[k, i, c, 0:1, :] = low
                slabs[k, i, c, rows + 1 : rows + 2, :] = high
        low, high = arrived(even_2, odd_2, rows_odd, (slice(0, depth), cols(c)))
        second[c, block.along(-1), :] = low
        second[c, block.along(rows), :] = high
    for k, d in ((0, -2), (1, depth + 1)):
        above, below = block.slab(first, -1, d, rows), block.slab(first, 1, d, rows)
        for c in every:
            partly = arrived(even_d, odd_d, depth_odd, (6, slice(None), cols(c)))[k]
            weight = arrived(even_d, odd_d, depth_odd, (7, slice(None), cols(c)))[k]
            extra = jnp.where(row == 0, above[c], jnp.where(row == rows - 1, below[c], 0.0))
            second[c, block.across(0, d, rows), :] = partly + weight * extra
    for k, d in ((0, -1), (1, depth)):
        values = block.section_slab(
            first, -1, d, rows + 2, lambda c: [slabs[k, i, c, 0 : rows + 2, :] for i in range(4)]
        )
        block.put(second, block.across(-1, d, rows + 2), values)

    for r in (0, rows - 1):
        values = block.section_line(second, r, lambda c: coef_of(diff, vel, r, c))
        block.put(third, block.along(r), values)
        for c in every:
            front[r, :, cols(c)] = values[c]
    save = pltpu.make_async_copy(front, front_far, sem)
    save.start()
    for k, r, inner in ((0, -1, 0), (1, rows, rows - 1)):
        for c in every:
            partly = arrived(even_2, odd_2, rows_odd, (slice(depth, 2 * depth), cols(c)))[k]
            weight = arrived(even_r, odd_r, rows_odd, (1, slice(None), cols(c)))[k]
            third[c, block.along(r), :] = partly + weight * second[c, block.along(inner), :]
            for side, d, past in ((0, 0, -1), (1, depth - 1, depth)):
                place = pl.ds(block.at(r, d), 1)
                more = corner(side, 7, c)[k] * second[c, pl.ds(block.at(r, past), 1), :]
                third[c, place, :] = third[c, place, :] + more
    for k, d in ((0, -1), (1, depth)):
        values = block.section_slab(
            second, 0, d, rows, lambda c: [slabs[k, i, c, 1 : rows + 1, :] for i in range(4)]
        )
        block.put(third, block.across(0, d, rows), values)

    def shine(d, carry):
        center = block.slab(third, 0, d, rows)
        before, after = beside(center)
        above, below = block.slab(third, -1, d, rows), block.slab(third, 1, d, rows)
        shallow, deep = block.slab(third, 0, d - 1, rows), block.slab(third, 0, d + 1, rows)
        result = []
        for c in every:
            through, total, red, green = carry[c]
            u = center[c]
            grad_row = below[c] - above[c]
            grad_deep = deep[c] - shallow[c]
            grad_col = after[c] - before[c]
            lighting = 0.48 * grad_row + 0.64 * grad_deep + 0.6 * grad_col
            magnitude = grad_row * grad_row + grad_deep * grad_deep + grad_col * grad_col + 0.4
            shade = 0.35 + 0.65 * lighting * lighting / magnitude
            passed = jnp.exp(-opacity * u)
            weight = through * (1.0 - passed) * shade
            colored = weight * u
            result.append((through * passed, total + weight, red + colored, green + colored * u))
        return tuple(result)

    zero, one = jnp.zeros((rows, lanes), jnp.float32), jnp.ones((rows, lanes), jnp.float32)
    carry = tuple((one, zero, zero, zero) for _ in every)
    for d in range(depth):
        carry = shine(d, carry)
    for c, (through, total, red, green) in enumerate(carry):
        partial[0, :, cols(c)] = red
        partial[1, :, cols(c)] = green
        partial[2, :, cols(c)] = total - red
        partial[3, :, cols(c)] = through
    save.wait()


def vmem(shape):
    return pltpu.VMEM(shape, jnp.float32)


def here(value):
    return pltpu.with_memory_space_constraint(value, pltpu.VMEM)


def far(value):
    return pltpu.with_memory_space_constraint(value, pltpu.HBM)


def shards(field, diffusivity, velocity):
    rows, depth, width = field.shape
    count = width // lanes
    block = Block(rows, depth, width)
    groups = lax.axis_size("depth")
    params = pltpu.CompilerParams(vmem_limit_bytes=24 * 2**20)
    in_hbm = pl.BlockSpec(memory_space=pltpu.HBM)

    own_types = [pltpu.VMEM(x.shape, x.dtype) for x in (field, diffusivity, velocity)]
    *own, even_d, odd_d, even_r, odd_r = pl.pallas_call(
        pack_kernel,
        in_specs=[in_hbm] * 3,
        out_shape=own_types + [vmem((8, rows, width))] * 2 + [vmem((2, depth, width))] * 2,
        scratch_shapes=[
            vmem((count, rows * depth, lanes)),
            vmem((4, count, rows * depth, lanes)),
            pltpu.SemaphoreType.DMA((3,)),
        ],
        compiler_params=params,
        name="pack",
    )(far(field), far(diffusivity), far(velocity))
    odd_r = here(swap_pairs(odd_r, "rows", 1))
    even_d = here(swap_pairs(even_d, "depth", 0))
    odd_d = here(swap_pairs(odd_d, "depth", 1))
    even_r = here(swap_pairs(even_r, "rows", 0))
    own = [here(x) for x in own]
    even_2, odd_2, middles = pl.pallas_call(
        edge_kernel,
        out_shape=[vmem((2 * depth + 16, width))] * 2 + [vmem((4, depth, width))],
        scratch_shapes=[
            vmem((4, count, block.pitch, lanes)),
            vmem((2, count, block.pitch, lanes)),
        ],
        compiler_params=params,
        name="edge",
    )(*own, even_d, odd_d, even_r, odd_r)
    even_2 = here(swap_pairs(even_2, "rows", 0))
    odd_2 = here(swap_pairs(odd_2, "rows", 1))
    held = [vmem((count, (rows + 4) * block.pitch, lanes))] * 3
    held += [vmem((2, 4, count, rows + 8, lanes)), vmem(field.shape)]
    state = pl.pallas_call(
        inner_kernel,
        out_shape=held,
        compiler_params=params,
        cost_estimate=pl.CostEstimate(
            flops=80 * field.size, bytes_accessed=8 * field.size, transcendentals=0
        ),
        name="inner",
    )(*own, even_d, odd_d, even_r, odd_r, here(middles))
    opacity = opacity_total / (depth * groups)
    *_, front, partial = pl.pallas_call(
        lambda *refs: rim_kernel(opacity, *refs),
        out_shape=held + [jax.ShapeDtypeStruct(field.shape, jnp.float32), vmem((4, rows, width))],
        out_specs=[pl.BlockSpec(memory_space=pltpu.VMEM)] * 5
        + [in_hbm, pl.BlockSpec(memory_space=pltpu.VMEM)],
        scratch_shapes=[pltpu.SemaphoreType.DMA],
        input_output_aliases={8 + i: i for i in range(5)},
        compiler_params=params,
        name="rim",
    )(*own[1:], even_d, odd_d, even_r, odd_r, even_2, odd_2, *[here(x) for x in state])

    position = lax.axis_index("depth")
    split = partial.reshape(4, rows, groups, width // groups)
    parts = []
    for apart in range(groups):
        part = lax.dynamic_index_in_dim(split, position ^ apart, 2, keepdims=False)
        if apart:
            part = lax.ppermute(part, "depth", [(i, i ^ apart) for i in range(groups)])
        parts.append(part)
    parts = jnp.stack(parts)
    picture = None
    for s in range(groups):
        segment = lax.dynamic_index_in_dim(parts, position ^ s, 0, keepdims=False)
        if picture is None:
            colors, through = segment[:3], segment[3:]
            picture = (colors, through)
        else:
            colors = colors + through * segment[:3]
            through = through * segment[3:]
    return front, jnp.concatenate([colors, through], axis=0)


def solution(mesh):
    return jax.shard_map(
        shards,
        mesh=mesh,
        in_specs=(
            P("rows", "depth", None),
            P("rows", "depth", None),
            P(None, "rows", "depth", None),
        ),
        out_specs=(P("rows", "depth", None), P(None, "rows", "depth")),
        check_vma=False,
    )
```

```python
import jax
import jax.numpy as jnp
from jax import lax
from jax.experimental import pallas as pl
from jax.experimental.pallas import tpu as pltpu
from jax.sharding import PartitionSpec as P

time_step = 0.2
growth_rate = 1.0
opacity_total = 3.0

lanes = 128
margin = 8


def pairs(count, first):
    forward = [(i, i + 1) for i in range(first, count - 1, 2)]
    return forward + [(target, source) for source, target in forward]


def swap_pairs(value, axis, first):
    return lax.ppermute(value, axis, pairs(lax.axis_size(axis), first))


def stencil(u, low, high, coef):
    diff = coef[0]
    change = growth_rate * u * (1.0 - u)
    for before, after, speed in zip(low, high, coef[1:]):
        change = change + (diff + jnp.maximum(speed, 0.0)) * (before - u)
        change = change + (diff - jnp.minimum(speed, 0.0)) * (after - u)
    return u + time_step * change


def beside(chunks):
    lane = lax.broadcasted_iota(jnp.int32, chunks[0].shape, 1)
    right = [pltpu.roll(x, 1, 1) for x in chunks]
    left = [pltpu.roll(x, lanes - 1, 1) for x in chunks]
    zero = jnp.zeros_like(chunks[0])
    count = len(chunks)
    before = [jnp.where(lane == 0, right[c - 1] if c else zero, right[c]) for c in range(count)]
    after = [
        jnp.where(lane == lanes - 1, left[c + 1] if c + 1 < count else zero, left[c])
        for c in range(count)
    ]
    return before, after


def cols(c):
    return slice(c * lanes, (c + 1) * lanes)


def coef_of(diff, vel, r, c):
    return [diff[r, :, cols(c)].astype(jnp.float32)] + [
        vel[i, r, :, cols(c)].astype(jnp.float32) for i in range(3)
    ]


def weight_low(diff, speed):
    return time_step * (diff + jnp.maximum(speed, 0.0))


def weight_high(diff, speed):
    return time_step * (diff - jnp.minimum(speed, 0.0))


def pack_kernel(
    field_far, diff_far, vel_far, field, diff, vel, even_d, odd_d, odd_r, even_r, flat, coefs, sems
):
    loads = [
        pltpu.make_async_copy(source, target, sems.at[i])
        for i, (source, target) in enumerate(
            ((field_far, field), (diff_far, diff), (vel_far, vel))
        )
    ]
    for load in loads:
        load.start()
    for load in loads:
        load.wait()
    rows, depth, width = field.shape
    pitch = depth + 4
    count = width // lanes
    depth_odd = lax.axis_index("depth") % 2 == 1
    rows_odd = lax.axis_index("rows") % 2 == 1

    for c in range(count):
        for r in range(rows):
            place = pl.ds(r * pitch, depth)
            coef = coef_of(diff, vel, r, c)
            flat[c, place, :] = field[r, :, cols(c)]
            for i in range(4):
                coefs[i, c, place, :] = coef[i]
            if r == 0:
                first = (field[r, :, cols(c)], weight_low(coef[0], coef[1]))
            if r == rows - 1:
                last = (field[r, :, cols(c)], weight_high(coef[0], coef[1]))
        for i in range(2):
            even_r[i, :, cols(c)] = jnp.where(rows_odd, first[i], last[i])
            odd_r[i, :, cols(c)] = jnp.where(rows_odd, last[i], first[i])

    row = lax.broadcasted_iota(jnp.int32, (rows, lanes), 0)
    sides = []
    for near, step in ((0, 1), (depth - 1, -1)):

        def slab(ref, d):
            return [ref[c, pl.ds(d, rows, stride=pitch), :] for c in range(count)]

        u0, u1, u2 = (slab(flat, near + step * j) for j in range(3))
        near_coef = [slab(coefs.at[i], near) for i in range(4)]
        next_coef = [slab(coefs.at[i], near + step) for i in range(4)]
        before, after = beside(u1)
        side = []
        for c in range(count):
            above = jnp.where(row == 0, 0.0, pltpu.roll(u1[c], 1, 0))
            below = jnp.where(row == rows - 1, 0.0, pltpu.roll(u1[c], rows - 1, 0))
            deep = (u0[c], u2[c]) if step > 0 else (u2[c], u0[c])
            coef = [next_coef[i][c] for i in range(4)]
            middle = stencil(
                u1[c], (above, deep[0], before[c]), (below, deep[1], after[c]), coef
            )
            weight = jnp.where(
                row == 0, weight_low(coef[0], coef[1]), weight_high(coef[0], coef[1])
            )
            side.append([u0[c], u1[c]] + [near_coef[i][c] for i in range(4)] + [middle, weight])
        sides.append(side)
    low, high = sides
    for c in range(count):
        for i in range(8):
            even_d[i, :, cols(c)] = jnp.where(depth_odd, low[c][i], high[c][i])
            odd_d[i, :, cols(c)] = jnp.where(depth_odd, high[c][i], low[c][i])


def arrived(even, odd, is_odd, index):
    a, b = even[index], odd[index]
    return jnp.where(is_odd, a, b), jnp.where(is_odd, b, a)


def edge_kernel(
    field, diff, vel, even_d, odd_d, odd_r, even_r, odd_2, even_2, middles, ext, edge
):
    rows, depth, width = field.shape
    every = range(width // lanes)
    depth_odd = lax.axis_index("depth") % 2 == 1
    rows_odd = lax.axis_index("rows") % 2 == 1
    own = pl.ds(margin, depth)
    shallow, deep = pl.ds(margin - 1, depth), pl.ds(margin + 1, depth)
    beyond = [arrived(even_r, odd_r, rows_odd, (0, slice(None), cols(c))) for c in every]
    lines = (0, 1, rows - 2, rows - 1)
    values = {r: [field[r, :, cols(c)] for c in every] for r in lines + (2, rows - 3)}
    values[-1] = [x[0] for x in beyond]
    values[rows] = [x[1] for x in beyond]
    coefs = {r: [coef_of(diff, vel, r, c) for c in every] for r in lines}
    for j, r in enumerate(lines):
        u = values[r]
        before, after = beside(u)
        for c in every:
            low, high = arrived(even_d, odd_d, depth_odd, (0, pl.ds(r, 1), cols(c)))
            ext[j, c, margin - 1 : margin, :] = low
            ext[j, c, own, :] = u[c]
            ext[j, c, margin + depth : margin + depth + 1, :] = high
        for c in every:
            middles[j, :, cols(c)] = stencil(
                u[c],
                (values[r - 1][c], ext[j, c, shallow, :], before[c]),
                (values[r + 1][c], ext[j, c, deep, :], after[c]),
                coefs[r][c],
            )
    zero = jnp.zeros((1, lanes), jnp.float32)
    none = jnp.zeros((depth, lanes), jnp.float32)
    sides = []
    for j, inner, r in ((0, 1, 0), (3, 2, rows - 1)):
        u = [middles[j, :, cols(c)] for c in every]
        before, after = beside(u)
        side = []
        for c in every:
            edge[j // 3, c, margin - 1 : margin, :] = zero
            edge[j // 3, c, own, :] = u[c]
            edge[j // 3, c, margin + depth : margin + depth + 1, :] = zero
        for c in every:
            next_row = middles[inner, :, cols(c)]
            above, below = (none, next_row) if r == 0 else (next_row, none)
            coef = coefs[r][c]
            partly = stencil(
                u[c],
                (above, edge[j // 3, c, shallow, :], before[c]),
                (below, edge[j // 3, c, deep, :], after[c]),
                coef,
            )
            side.append(
                (u[c], partly, weight_low(coef[0], coef[2]), weight_high(coef[0], coef[2]))
            )
        sides.append(side)
    first, last = sides
    for c in every:
        for i in range(2):
            place = pl.ds(i * depth, depth)
            even_2[place, cols(c)] = jnp.where(rows_odd, first[c][i], last[c][i])
            odd_2[place, cols(c)] = jnp.where(rows_odd, last[c][i], first[c][i])
        for k, d in ((0, 0), (1, depth - 1)):
            place = 2 * depth + 8 * k + 7
            f_val, l_val = first[c][2 + k][d : d + 1], last[c][2 + k][d : d + 1]
            even_2[place : place + 1, cols(c)] = jnp.where(rows_odd, f_val, l_val)
            odd_2[place : place + 1, cols(c)] = jnp.where(rows_odd, l_val, f_val)
    for j, (item, f_row) in enumerate(
        ((0, 0), (1, 0), (0, 1), (2, 0), (3, 0), (4, 0), (5, 0))
    ):
        l_row = rows - 1 - f_row
        for c in every:
            f_both = arrived(even_d, odd_d, depth_odd, (item, pl.ds(f_row, 1), cols(c)))
            l_both = arrived(even_d, odd_d, depth_odd, (item, pl.ds(l_row, 1), cols(c)))
            for k in range(2):
                place = 2 * depth + 8 * k + j
                even_2[place : place + 1, cols(c)] = jnp.where(rows_odd, f_both[k], l_both[k])
                odd_2[place : place + 1, cols(c)] = jnp.where(rows_odd, l_both[k], f_both[k])


class Block:
    def __init__(self, rows, depth, width):
        self.rows, self.depth, self.every = rows, depth, range(width // lanes)
        self.pitch = depth + 2 * margin + 1

    def at(self, r, d):
        return (r + 2) * self.pitch + margin + d

    def along(self, r, d=0):
        return pl.ds(self.at(r, d), self.depth)

    def across(self, r, d, length):
        return pl.ds(self.at(r, d), length, stride=self.pitch)

    def line(self, ref, r, d=0):
        return [ref[c, self.along(r, d), :] for c in self.every]

    def slab(self, ref, r, d, length):
        return [ref[c, self.across(r, d, length), :] for c in self.every]

    def put(self, ref, place, values):
        for c in self.every:
            ref[c, place, :] = values[c]

    def section_line(self, ref, r, coef):
        u = self.line(ref, r)
        before, after = beside(u)
        low = (self.line(ref, r - 1), self.line(ref, r, -1), before)
        high = (self.line(ref, r + 1), self.line(ref, r, 1), after)
        return [
            stencil(u[c], [x[c] for x in low], [x[c] for x in high], coef(c)) for c in self.every
        ]

    def section_slab(self, ref, r, d, length, coef):
        u = self.slab(ref, r, d, length)
        before, after = beside(u)
        low = (self.slab(ref, r - 1, d, length), self.slab(ref, r, d - 1, length), before)
        high = (self.slab(ref, r + 1, d, length), self.slab(ref, r, d + 1, length), after)
        return [
            stencil(u[c], [x[c] for x in low], [x[c] for x in high], coef(c)) for c in self.every
        ]


def inner_kernel(
    field, diff, vel, even_d, odd_d, odd_r, even_r, middles, first, second, third, slabs, front
):
    rows, depth, width = field.shape
    block = Block(rows, depth, width)
    depth_odd = lax.axis_index("depth") % 2 == 1
    rows_odd = lax.axis_index("rows") % 2 == 1
    for c in block.every:
        for r in range(rows):
            first[c, block.along(r), :] = field[r, :, cols(c)]
        low, high = arrived(even_r, odd_r, rows_odd, (0, slice(None), cols(c)))
        first[c, block.along(-1), :] = low
        first[c, block.along(rows), :] = high
        for j in range(2):
            low, high = arrived(even_d, odd_d, depth_odd, (j, slice(None), cols(c)))
            first[c, block.across(0, -1 - j, rows), :] = low
            first[c, block.across(0, depth + j, rows), :] = high
        for i in range(4):
            both = arrived(even_d, odd_d, depth_odd, (2 + i, slice(None), cols(c)))
            for k in range(2):
                slabs[k, i, c, 1 : rows + 1, :] = both[k]
        for j, r in enumerate((0, 1, rows - 2, rows - 1)):
            second[c, block.along(r), :] = middles[j, :, cols(c)]

    def own_middle(r, carry):
        values = block.section_line(first, r, lambda c: coef_of(diff, vel, r, c))
        block.put(second, block.along(r), values)
        return carry

    lax.fori_loop(2, rows - 2, own_middle, 0)
    for k, d in ((0, -1), (1, depth)):
        values = block.section_slab(
            first, 1, d, rows - 2, lambda c: [slabs[k, i, c, 2:rows, :] for i in range(4)]
        )
        block.put(second, block.across(1, d, rows - 2), values)

    def own_front(r, carry):
        values = block.section_line(second, r, lambda c: coef_of(diff, vel, r, c))
        block.put(third, block.along(r), values)
        for c in block.every:
            front[r, :, cols(c)] = values[c]
        return carry

    lax.fori_loop(1, rows - 1, own_front, 0)


def rim_kernel(
    opacity, diff, vel, even_d, odd_d, odd_r, even_r, odd_2, even_2, *refs
):
    first, second, third, slabs, front, front_far, partial, sem = refs[5:]
    rows, depth, width = front.shape
    block = Block(rows, depth, width)
    every = block.every
    depth_odd = lax.axis_index("depth") % 2 == 1
    rows_odd = lax.axis_index("rows") % 2 == 1
    row = lax.broadcasted_iota(jnp.int32, (rows, lanes), 0)

    def corner(k, j, c):
        place = 2 * depth + 8 * k + j
        return arrived(even_2, odd_2, rows_odd, (slice(place, place + 1), cols(c)))

    for c in every:
        for k, step in ((0, -1), (1, 1)):
            near = -1 if k == 0 else depth
            for j, r, d in ((0, 1, near), (1, 1, near + step), (2, 2, near)):
                low, high = corner(k, j, c)
                first[c, pl.ds(block.at(-r, d), 1), :] = low
                first[c, pl.ds(block.at(rows - 1 + r, d), 1), :] = high
            for i in range(4):
                low, high = corner(k, 3 + i, c)
                slabs[k, i, c, 0:1, :] = low
                slabs[k, i, c, rows + 1 : rows + 2, :] = high
        low, high = arrived(even_2, odd_2, rows_odd, (slice(0, depth), cols(c)))
        second[c, block.along(-1), :] = low
        second[c, block.along(rows), :] = high
    for k, d in ((0, -2), (1, depth + 1)):
        above, below = block.slab(first, -1, d, rows), block.slab(first, 1, d, rows)
        for c in every:
            partly = arrived(even_d, odd_d, depth_odd, (6, slice(None), cols(c)))[k]
            weight = arrived(even_d, odd_d, depth_odd, (7, slice(None), cols(c)))[k]
            extra = jnp.where(row == 0, above[c], jnp.where(row == rows - 1, below[c], 0.0))
            second[c, block.across(0, d, rows), :] = partly + weight * extra
    for k, d in ((0, -1), (1, depth)):
        values = block.section_slab(
            first, -1, d, rows + 2, lambda c: [slabs[k, i, c, 0 : rows + 2, :] for i in range(4)]
        )
        block.put(second, block.across(-1, d, rows + 2), values)

    for r in (0, rows - 1):
        values = block.section_line(second, r, lambda c: coef_of(diff, vel, r, c))
        block.put(third, block.along(r), values)
        for c in every:
            front[r, :, cols(c)] = values[c]
    save = pltpu.make_async_copy(front, front_far, sem)
    save.start()
    for k, r, inner in ((0, -1, 0), (1, rows, rows - 1)):
        for c in every:
            partly = arrived(even_2, odd_2, rows_odd, (slice(depth, 2 * depth), cols(c)))[k]
            weight = arrived(even_r, odd_r, rows_odd, (1, slice(None), cols(c)))[k]
            third[c, block.along(r), :] = partly + weight * second[c, block.along(inner), :]
            for side, d, past in ((0, 0, -1), (1, depth - 1, depth)):
                place = pl.ds(block.at(r, d), 1)
                more = corner(side, 7, c)[k] * second[c, pl.ds(block.at(r, past), 1), :]
                third[c, place, :] = third[c, place, :] + more
    for k, d in ((0, -1), (1, depth)):
        values = block.section_slab(
            second, 0, d, rows, lambda c: [slabs[k, i, c, 1 : rows + 1, :] for i in range(4)]
        )
        block.put(third, block.across(0, d, rows), values)

    def shine(d, carry):
        shallow, center, deep = planes[d], planes[d + 1], planes[d + 2]
        before, after = beside(center)
        above, below = block.slab(third, -1, d, rows), block.slab(third, 1, d, rows)
        result = []
        for c in every:
            through, total, red, green = carry[c]
            u = center[c]
            grad_row = below[c] - above[c]
            grad_deep = deep[c] - shallow[c]
            grad_col = after[c] - before[c]
            lighting = 0.48 * grad_row + 0.64 * grad_deep + 0.6 * grad_col
            magnitude = grad_row * grad_row + grad_deep * grad_deep + grad_col * grad_col + 0.4
            shade = 0.35 + 0.65 * lighting * lighting / magnitude
            passed = jnp.exp(-opacity * u)
            weight = through * (1.0 - passed) * shade
            colored = weight * u
            result.append((through * passed, total + weight, red + colored, green + colored * u))
        return tuple(result)

    zero, one = jnp.zeros((rows, lanes), jnp.float32), jnp.ones((rows, lanes), jnp.float32)
    carry = tuple((one, zero, zero, zero) for _ in every)
    planes = [block.slab(third, 0, -1, rows), block.slab(third, 0, 0, rows)]
    for d in range(depth):
        planes.append(block.slab(third, 0, d + 1, rows))
        carry = shine(d, carry)
    for c, (through, total, red, green) in enumerate(carry):
        partial[0, :, cols(c)] = red
        partial[1, :, cols(c)] = green
        partial[2, :, cols(c)] = total - red
        partial[3, :, cols(c)] = through
    save.wait()


def vmem(shape):
    return pltpu.VMEM(shape, jnp.float32)


def here(value):
    return pltpu.with_memory_space_constraint(value, pltpu.VMEM)


def far(value):
    return pltpu.with_memory_space_constraint(value, pltpu.HBM)


def shards(field, diffusivity, velocity):
    rows, depth, width = field.shape
    count = width // lanes
    block = Block(rows, depth, width)
    groups = lax.axis_size("depth")
    params = pltpu.CompilerParams(vmem_limit_bytes=24 * 2**20)
    in_hbm = pl.BlockSpec(memory_space=pltpu.HBM)

    own_types = [pltpu.VMEM(x.shape, x.dtype) for x in (field, diffusivity, velocity)]
    *own, even_d, odd_d, odd_r, even_r = pl.pallas_call(
        pack_kernel,
        in_specs=[in_hbm] * 3,
        out_shape=own_types + [vmem((8, rows, width))] * 2 + [vmem((2, depth, width))] * 2,
        scratch_shapes=[
            vmem((count, rows * (depth + 4), lanes)),
            vmem((4, count, rows * (depth + 4), lanes)),
            pltpu.SemaphoreType.DMA((3,)),
        ],
        compiler_params=params,
        name="pack",
    )(far(field), far(diffusivity), far(velocity))
    odd_r = here(swap_pairs(odd_r, "rows", 1))
    even_d = here(swap_pairs(even_d, "depth", 0))
    odd_d = here(swap_pairs(odd_d, "depth", 1))
    even_r = here(swap_pairs(even_r, "rows", 0))
    own = [here(x) for x in own]
    odd_2, even_2, middles = pl.pallas_call(
        edge_kernel,
        out_shape=[vmem((2 * depth + 16, width))] * 2 + [vmem((4, depth, width))],
        scratch_shapes=[
            vmem((4, count, depth + 2 * margin, lanes)),
            vmem((2, count, depth + 2 * margin, lanes)),
        ],
        compiler_params=params,
        name="edge",
    )(*own, even_d, odd_d, odd_r, even_r)
    odd_2 = here(swap_pairs(odd_2, "rows", 1))
    even_2 = here(swap_pairs(even_2, "rows", 0))
    held = [vmem((count, (rows + 4) * block.pitch + margin, lanes))] * 3
    held += [vmem((2, 4, count, rows + 8, lanes)), vmem(field.shape)]
    state = pl.pallas_call(
        inner_kernel,
        out_shape=held,
        compiler_params=params,
        cost_estimate=pl.CostEstimate(
            flops=80 * field.size, bytes_accessed=8 * field.size, transcendentals=0
        ),
        name="inner",
    )(*own, even_d, odd_d, odd_r, even_r, here(middles))
    opacity = opacity_total / (depth * groups)
    *_, front, partial = pl.pallas_call(
        lambda *refs: rim_kernel(opacity, *refs),
        out_shape=held + [jax.ShapeDtypeStruct(field.shape, jnp.float32), vmem((4, rows, width))],
        out_specs=[pl.BlockSpec(memory_space=pltpu.VMEM)] * 5
        + [in_hbm, pl.BlockSpec(memory_space=pltpu.VMEM)],
        scratch_shapes=[pltpu.SemaphoreType.DMA],
        input_output_aliases={8 + i: i for i in range(5)},
        compiler_params=params,
        name="rim",
    )(*own[1:], even_d, odd_d, odd_r, even_r, odd_2, even_2, *[here(x) for x in state])

    position = lax.axis_index("depth")
    split = partial.reshape(4, rows, groups, width // groups)
    parts = {}
    for apart in range(groups):
        part = lax.dynamic_index_in_dim(split, position ^ apart, 2, keepdims=False)
        if apart:
            part = lax.ppermute(part, "depth", [(i, i ^ apart) for i in range(groups)])
        parts[apart] = part
    parts = jnp.stack([parts[-apart % groups] for apart in range(groups)])
    picture = None
    for s in range(groups):
        apart = position ^ s
        segment = lax.dynamic_index_in_dim(parts, -apart % groups, 0, keepdims=False)
        if picture is None:
            colors, through = segment[:3], segment[3:]
            picture = (colors, through)
        else:
            colors = colors + through * segment[:3]
            through = through * segment[3:]
    return front, jnp.concatenate([colors, through], axis=0)


def solution(mesh):
    return jax.shard_map(
        shards,
        mesh=mesh,
        in_specs=(
            P("rows", "depth", None),
            P("rows", "depth", None),
            P(None, "rows", "depth", None),
        ),
        out_specs=(P("rows", "depth", None), P(None, "rows", "depth")),
        check_vma=False,
    )
```

```python
import jax
import jax.numpy as jnp
from jax import lax
from jax.experimental import pallas as pl
from jax.experimental.pallas import tpu as pltpu
from jax.sharding import PartitionSpec as P

time_step = 0.2
growth_rate = 1.0
opacity_total = 3.0

lanes = 128
margin = 8
pack_gap = 4


def pairs(count, first):
    forward = [(i, i + 1) for i in range(first, count - 1, 2)]
    return forward + [(target, source) for source, target in forward]


def swap_pairs(value, axis, first):
    return lax.ppermute(value, axis, pairs(lax.axis_size(axis), first))


def stencil(u, low, high, coef):
    diff = coef[0]
    change = growth_rate * u * (1.0 - u)
    for before, after, speed in zip(low, high, coef[1:]):
        change = change + (diff + jnp.maximum(speed, 0.0)) * (before - u)
        change = change + (diff - jnp.minimum(speed, 0.0)) * (after - u)
    return u + time_step * change


def beside(chunks):
    lane = lax.broadcasted_iota(jnp.int32, chunks[0].shape, 1)
    right = [pltpu.roll(x, 1, 1) for x in chunks]
    left = [pltpu.roll(x, lanes - 1, 1) for x in chunks]
    zero = jnp.zeros_like(chunks[0])
    count = len(chunks)
    before = [jnp.where(lane == 0, right[c - 1] if c else zero, right[c]) for c in range(count)]
    after = [
        jnp.where(lane == lanes - 1, left[c + 1] if c + 1 < count else zero, left[c])
        for c in range(count)
    ]
    return before, after


def cols(c):
    return slice(c * lanes, (c + 1) * lanes)


def coef_of(diff, vel, r, c):
    return [diff[r, :, cols(c)].astype(jnp.float32)] + [
        vel[i, r, :, cols(c)].astype(jnp.float32) for i in range(3)
    ]


def weight_low(diff, speed):
    return time_step * (diff + jnp.maximum(speed, 0.0))


def weight_high(diff, speed):
    return time_step * (diff - jnp.minimum(speed, 0.0))


def pack_kernel(
    field_far, diff_far, vel_far, field, diff, vel, even_d, odd_d, odd_f, near, flat, coefs, sems
):
    loads = [
        pltpu.make_async_copy(source, target, sems.at[i])
        for i, (source, target) in enumerate(
            ((field_far, field), (diff_far, diff), (vel_far, vel))
        )
    ]
    for load in loads:
        load.start()
    for load in loads:
        load.wait()
    rows, depth, width = field.shape
    count = width // lanes
    pitch = depth + pack_gap
    depth_odd = lax.axis_index("depth") % 2 == 1
    rows_odd = lax.axis_index("rows") % 2 == 1

    for c in range(count):
        for r in range(rows):
            place = pl.ds(r * pitch, depth)
            coef = coef_of(diff, vel, r, c)
            flat[c, place, :] = field[r, :, cols(c)]
            for i in range(4):
                coefs[i, c, place, :] = coef[i]
        first, last = field[0, :, cols(c)], field[rows - 1, :, cols(c)]
        odd_f[:, cols(c)] = jnp.where(rows_odd, last, first)

    row = lax.broadcasted_iota(jnp.int32, (rows, lanes), 0)
    sides = []
    for k, start, step in ((0, 0, 1), (1, depth - 1, -1)):

        def slab(ref, d):
            return [ref[c, pl.ds(d, rows, stride=pitch), :] for c in range(count)]

        u0, u1, u2 = (slab(flat, start + step * j) for j in range(3))
        near_coef = [slab(coefs.at[i], start) for i in range(4)]
        next_coef = [slab(coefs.at[i], start + step) for i in range(4)]
        before, after = beside(u1)
        side = []
        for c in range(count):
            near[k, :, cols(c)] = u0[c]
            above, below = past_rows(u1[c], row)
            deep = (u0[c], u2[c]) if step > 0 else (u2[c], u0[c])
            coef = [next_coef[i][c] for i in range(4)]
            middle = stencil(
                u1[c], (above, deep[0], before[c]), (below, deep[1], after[c]), coef
            )
            weight = row_weight(row, coef)
            side.append([u0[c], u1[c]] + [near_coef[i][c] for i in range(4)] + [middle, weight])
        sides.append(side)
    low, high = sides
    for c in range(count):
        for i in range(8):
            even_d[i, :, cols(c)] = jnp.where(depth_odd, low[c][i], high[c][i])
            odd_d[i, :, cols(c)] = jnp.where(depth_odd, high[c][i], low[c][i])


def spare_kernel(field, diff, vel, odd_x, even_x, partial, own_w, own_d, ext):
    rows, depth, width = field.shape
    every = range(width // lanes)
    rows_odd = lax.axis_index("rows") % 2 == 1
    own = pl.ds(margin, depth)
    shallow, deep = pl.ds(margin - 1, depth), pl.ds(margin + 1, depth)
    none = jnp.zeros((depth, lanes), jnp.float32)
    zero = jnp.zeros((1, lanes), jnp.float32)
    for j, r in enumerate((0, 1, rows - 2, rows - 1)):
        u = [field[r, :, cols(c)] for c in every]
        before, after = beside(u)
        for c in every:
            ext[j, c, margin - 1 : margin, :] = zero
            ext[j, c, own, :] = u[c]
            ext[j, c, margin + depth : margin + depth + 1, :] = zero
        for c in every:
            above = field[r - 1, :, cols(c)] if r > 0 else none
            below = field[r + 1, :, cols(c)] if r < rows - 1 else none
            coef = coef_of(diff, vel, r, c)
            partial[j, :, cols(c)] = stencil(
                u[c],
                (above, ext[j, c, shallow, :], before[c]),
                (below, ext[j, c, deep, :], after[c]),
                coef,
            )
            low = weight_low(coef[0], coef[2])[0:1]
            high = weight_high(coef[0], coef[2])[depth - 1 : depth]
            own_d[2 * j : 2 * j + 1, cols(c)] = low
            own_d[2 * j + 1 : 2 * j + 2, cols(c)] = high
            if r == 0:
                own_w[0, :, cols(c)] = weight_low(coef[0], coef[1])
            if r == rows - 1:
                own_w[1, :, cols(c)] = weight_high(coef[0], coef[1])
    for c in every:
        first, last = field[0, :, cols(c)], field[rows - 1, :, cols(c)]
        even_x[:depth, cols(c)] = jnp.where(rows_odd, first, last)
        for start, length, low, high in (
            (0, depth, own_w[0, :, cols(c)], own_w[1, :, cols(c)]),
            (depth, depth, partial[0, :, cols(c)], partial[3, :, cols(c)]),
            (2 * depth, 2, own_d[0:2, cols(c)], own_d[6:8, cols(c)]),
        ):
            even_x[pl.ds(depth + start, length), cols(c)] = jnp.where(rows_odd, low, high)
            odd_x[pl.ds(start, length), cols(c)] = jnp.where(rows_odd, high, low)


def arrived(even, odd, is_odd, index, even_index=None):
    a, b = even[index if even_index is None else even_index], odd[index]
    return jnp.where(is_odd, a, b), jnp.where(is_odd, b, a)


def past_rows(u, row):
    rows = u.shape[0]
    above = jnp.where(row == 0, 0.0, pltpu.roll(u, 1, 0))
    below = jnp.where(row == rows - 1, 0.0, pltpu.roll(u, rows - 1, 0))
    return above, below


def row_weight(row, coef):
    return jnp.where(row == 0, weight_low(coef[0], coef[1]), weight_high(coef[0], coef[1]))


def at_ends(first, last, shape):
    place = lax.broadcasted_iota(jnp.int32, shape, 0)
    return jnp.where(place == 0, first, jnp.where(place == shape[0] - 1, last, 0.0))


def edge_kernel(
    diff, vel, even_d, odd_d, odd_f, even_x, near, partial, own_w, own_d,
    odd_2, even_2, middles, partly, sides, ext, stack,
):
    _, rows, width = even_d.shape
    depth = diff.shape[1]
    every = range(width // lanes)
    depth_odd = lax.axis_index("depth") % 2 == 1
    rows_odd = lax.axis_index("rows") % 2 == 1
    own = pl.ds(margin, depth)
    shallow, deep = pl.ds(margin - 1, depth), pl.ds(margin + 1, depth)
    row = lax.broadcasted_iota(jnp.int32, (rows, lanes), 0)
    none = jnp.zeros((depth, lanes), jnp.float32)
    zero = jnp.zeros((1, lanes), jnp.float32)
    lines = {j: [] for j in range(4)}
    for c in every:
        beyond = arrived(even_x, odd_f, rows_odd, (pl.ds(0, depth), cols(c)))
        for j, r in enumerate((0, 1, rows - 2, rows - 1)):
            value = partial[j, :, cols(c)]
            if j in (0, 3):
                value = value + own_w[j // 3, :, cols(c)] * beyond[j // 3]
            both = arrived(even_d, odd_d, depth_odd, (0, pl.ds(r, 1), cols(c)))
            weights = [own_d[2 * j + k : 2 * j + k + 1, cols(c)] for k in range(2)]
            value = value + at_ends(weights[0] * both[0], weights[1] * both[1], value.shape)
            lines[j].append(value)
            middles[j, :, cols(c)] = value
            if j in (0, 3):
                ext[j // 3, c, margin - 1 : margin, :] = zero
                ext[j // 3, c, own, :] = value
                ext[j // 3, c, margin + depth : margin + depth + 1, :] = zero
    for j, inner, r in ((0, 1, 0), (3, 2, rows - 1)):
        u = lines[j]
        before, after = beside(u)
        for c in every:
            next_row = lines[inner][c]
            above, below = (none, next_row) if r == 0 else (next_row, none)
            partly[j // 3, :, cols(c)] = stencil(
                u[c],
                (above, ext[j // 3, c, shallow, :], before[c]),
                (below, ext[j // 3, c, deep, :], after[c]),
                coef_of(diff, vel, r, c),
            )
    for c in every:
        first, last = partly[0, :, cols(c)], partly[1, :, cols(c)]
        even_2[:depth, cols(c)] = jnp.where(rows_odd, first, last)
        odd_2[:depth, cols(c)] = jnp.where(rows_odd, last, first)

    def came(item, c, k):
        return arrived(even_d, odd_d, depth_odd, (item, slice(None), cols(c)))[k]

    for k in range(2):
        u = [came(0, c, k) for c in every]
        before, after = beside(u)
        for c in every:
            above, below = past_rows(u[c], row)
            here_d, beyond_d = near[k, :, cols(c)], came(1, c, k)
            low_d, high_d = (beyond_d, here_d) if k == 0 else (here_d, beyond_d)
            coef = [came(2 + i, c, k) for i in range(4)]
            sides[k, 0, :, cols(c)] = stencil(
                u[c], (above, low_d, before[c]), (below, high_d, after[c]), coef
            )
            sides[k, 1, :, cols(c)] = row_weight(row, coef)
            values = (u[c], beyond_d, sides[k, 0, :, cols(c)], sides[k, 1, :, cols(c)])
            for j, value in enumerate(values):
                stack[c, pl.ds((4 * k + j) * (rows + 1), rows), :] = value
    for c in every:
        first = stack[c, pl.ds(0, 8, stride=rows + 1), :]
        last = stack[c, pl.ds(rows - 1, 8, stride=rows + 1), :]
        even_2[depth : depth + 8, cols(c)] = jnp.where(rows_odd, first, last)
        odd_2[depth : depth + 8, cols(c)] = jnp.where(rows_odd, last, first)


class Block:
    def __init__(self, rows, depth, width):
        self.rows, self.depth, self.every = rows, depth, range(width // lanes)
        self.pitch = depth + 2 * margin + 1

    def at(self, r, d):
        return (r + 2) * self.pitch + margin + d

    def along(self, r, d=0):
        return pl.ds(self.at(r, d), self.depth)

    def across(self, r, d, length):
        return pl.ds(self.at(r, d), length, stride=self.pitch)

    def line(self, ref, r, d=0):
        return [ref[c, self.along(r, d), :] for c in self.every]

    def slab(self, ref, r, d, length):
        return [ref[c, self.across(r, d, length), :] for c in self.every]

    def put(self, ref, place, values):
        for c in self.every:
            ref[c, place, :] = values[c]

    def section_line(self, ref, r, coef):
        u = self.line(ref, r)
        before, after = beside(u)
        low = (self.line(ref, r - 1), self.line(ref, r, -1), before)
        high = (self.line(ref, r + 1), self.line(ref, r, 1), after)
        return [
            stencil(u[c], [x[c] for x in low], [x[c] for x in high], coef(c)) for c in self.every
        ]

    def section_slab(self, ref, r, d, length, coef):
        u = self.slab(ref, r, d, length)
        before, after = beside(u)
        low = (self.slab(ref, r - 1, d, length), self.slab(ref, r, d - 1, length), before)
        high = (self.slab(ref, r + 1, d, length), self.slab(ref, r, d + 1, length), after)
        return [
            stencil(u[c], [x[c] for x in low], [x[c] for x in high], coef(c)) for c in self.every
        ]


def inner_kernel(
    field, diff, vel, even_d, odd_d, middles, sides,
    second, third, front_far, first, front, sem,
):
    rows, depth, width = field.shape
    block = Block(rows, depth, width)
    depth_odd = lax.axis_index("depth") % 2 == 1
    for c in block.every:
        for r in range(1, rows - 1):
            first[c, block.along(r), :] = field[r, :, cols(c)]
        low, high = arrived(even_d, odd_d, depth_odd, (0, slice(None), cols(c)))
        first[c, block.across(0, -1, rows), :] = low
        first[c, block.across(0, depth, rows), :] = high
        low, high = arrived(even_d, odd_d, depth_odd, (6, slice(None), cols(c)))
        second[c, block.across(0, -2, rows), :] = low
        second[c, block.across(0, depth + 1, rows), :] = high
        second[c, block.across(0, -1, rows), :] = sides[0, 0, :, cols(c)]
        second[c, block.across(0, depth, rows), :] = sides[1, 0, :, cols(c)]
        for j, r in enumerate((0, 1, rows - 2, rows - 1)):
            second[c, block.along(r), :] = middles[j, :, cols(c)]

    def own_middle(r, carry):
        values = block.section_line(first, r, lambda c: coef_of(diff, vel, r, c))
        block.put(second, block.along(r), values)
        return carry

    lax.fori_loop(2, rows - 2, own_middle, 0)

    def own_front(r, carry):
        values = block.section_line(second, r, lambda c: coef_of(diff, vel, r, c))
        block.put(third, block.along(r), values)
        for c in block.every:
            front[r, :, cols(c)] = values[c]
        return carry

    lax.fori_loop(1, rows - 1, own_front, 0)
    within = pl.ds(1, rows - 2)
    save = pltpu.make_async_copy(front.at[within], front_far.at[within], sem)
    save.start()
    save.wait()


def rim_kernel(
    opacity, field, even_d, odd_d, odd_x, even_x, odd_2, even_2, own_w, own_d, middles, partly, sides,
    *refs
):
    second, third, front_far, partial, front, sems = refs[3:]
    rows, depth, width = field.shape
    block = Block(rows, depth, width)
    every = block.every
    depth_odd = lax.axis_index("depth") % 2 == 1
    rows_odd = lax.axis_index("rows") % 2 == 1
    line = (depth, lanes)

    def spare(start, length, c):
        index = (slice(start, start + length), cols(c))
        shifted = (slice(depth + start, depth + start + length), cols(c))
        return arrived(even_x, odd_x, rows_odd, index, shifted)

    def corner(k, j, c):
        place = depth + 4 * k + j
        return arrived(even_2, odd_2, rows_odd, (slice(place, place + 1), cols(c)))

    def cell(ref, c, r, d, value):
        ref[c, pl.ds(block.at(r, d), 1), :] = value

    ends = ((0, 0, -1), (1, depth - 1, depth))
    rims = ((0, 0, -1), (1, rows - 1, rows))

    for c in every:
        weights, parts = spare(0, depth, c), spare(depth, depth, c)
        fronts = arrived(even_2, odd_2, rows_odd, (slice(0, depth), cols(c)))
        along = [spare(2 * depth + k, 1, c) for k in range(2)]
        corners = [[corner(k, j, c) for j in range(4)] for k in range(2)]
        for e, r, past in rims:
            near = [corners[k][0][e] for k in range(2)]
            middle = parts[e] + weights[e] * field[r, :, cols(c)]
            middle = middle + at_ends(along[0][e] * near[0], along[1][e] * near[1], line)
            second[c, block.along(past), :] = middle
            own_ends, past_ends = [], []
            for k, d, beyond in ends:
                index = (slice(r, r + 1), cols(c))
                outside = arrived(even_d, odd_d, depth_odd, (0, *index))[k]
                next_cell = arrived(even_d, odd_d, depth_odd, (6, *index))[k]
                next_weight = arrived(even_d, odd_d, depth_odd, (7, *index))[k]
                _, far_cell, part, weight = (x[e] for x in corners[k])
                past_ends.append(part + weight * outside)
                own_ends.append(sides[k, 0, *index] + sides[k, 1, *index] * near[k])
                cell(second, c, past, beyond, past_ends[k])
                cell(second, c, r, beyond, own_ends[k])
                cell(second, c, r, 2 * beyond - d, next_cell + next_weight * far_cell)
            own_along = [own_d[6 * e + k : 6 * e + k + 1, cols(c)] for k in range(2)]
            value = partly[e, :, cols(c)] + own_w[e, :, cols(c)] * middle
            value = value + at_ends(
                own_along[0] * own_ends[0], own_along[1] * own_ends[1], line
            )
            third[c, block.along(r), :] = value
            front[e, :, cols(c)] = value
            value = fronts[e] + weights[e] * middles[3 * e, :, cols(c)]
            third[c, block.along(past), :] = value + at_ends(
                along[0][e] * past_ends[0], along[1][e] * past_ends[1], line
            )
    saves = [
        pltpu.make_async_copy(front.at[e], front_far.at[r], sems.at[e]) for e, r, past in rims
    ]
    for save in saves:
        save.start()
    for k, d, beyond in ends:
        items = [
            [
                arrived(even_d, odd_d, depth_odd, (2 + i, slice(None), cols(c)))[k]
                for i in range(4)
            ]
            for c in every
        ]
        values = block.section_slab(second, 0, beyond, rows, lambda c: items[c])
        block.put(third, block.across(0, beyond, rows), values)

    def shine(d, carry):
        shallow, center, deep = planes[d], planes[d + 1], planes[d + 2]
        before, after = beside(center)
        above, below = block.slab(third, -1, d, rows), block.slab(third, 1, d, rows)
        result = []
        for c in every:
            through, total, red, green = carry[c]
            u = center[c]
            grad_row = below[c] - above[c]
            grad_deep = deep[c] - shallow[c]
            grad_col = after[c] - before[c]
            lighting = 0.48 * grad_row + 0.64 * grad_deep + 0.6 * grad_col
            magnitude = grad_row * grad_row + grad_deep * grad_deep + grad_col * grad_col + 0.4
            shade = 0.35 + 0.65 * lighting * lighting / magnitude
            passed = jnp.exp(-opacity * u)
            weight = through * (1.0 - passed) * shade
            colored = weight * u
            result.append((through * passed, total + weight, red + colored, green + colored * u))
        return tuple(result)

    zero, one = jnp.zeros((rows, lanes), jnp.float32), jnp.ones((rows, lanes), jnp.float32)
    carry = tuple((one, zero, zero, zero) for _ in every)
    planes = [block.slab(third, 0, -1, rows), block.slab(third, 0, 0, rows)]
    for d in range(depth):
        planes.append(block.slab(third, 0, d + 1, rows))
        carry = shine(d, carry)
    for c, (through, total, red, green) in enumerate(carry):
        partial[0, :, cols(c)] = red
        partial[1, :, cols(c)] = green
        partial[2, :, cols(c)] = total - red
        partial[3, :, cols(c)] = through
    for save in saves:
        save.wait()


def vmem(shape):
    return pltpu.VMEM(shape, jnp.float32)


def here(value):
    return pltpu.with_memory_space_constraint(value, pltpu.VMEM)


def far(value):
    return pltpu.with_memory_space_constraint(value, pltpu.HBM)


def shards(field, diffusivity, velocity):
    rows, depth, width = field.shape
    count = width // lanes
    block = Block(rows, depth, width)
    groups = lax.axis_size("depth")
    params = pltpu.CompilerParams(vmem_limit_bytes=24 * 2**20)
    in_hbm = pl.BlockSpec(memory_space=pltpu.HBM)

    own_types = [pltpu.VMEM(x.shape, x.dtype) for x in (field, diffusivity, velocity)]
    *own, even_d, odd_d, odd_f, near = pl.pallas_call(
        pack_kernel,
        in_specs=[in_hbm] * 3,
        out_shape=own_types
        + [vmem((8, rows, width))] * 2
        + [vmem((depth, width)), vmem((2, rows, width))],
        scratch_shapes=[
            vmem((count, rows * (depth + pack_gap), lanes)),
            vmem((4, count, rows * (depth + pack_gap), lanes)),
            pltpu.SemaphoreType.DMA((3,)),
        ],
        compiler_params=params,
        name="pack",
    )(far(field), far(diffusivity), far(velocity))
    odd_f = here(swap_pairs(odd_f, "rows", 1))
    even_d = here(swap_pairs(even_d, "depth", 0))
    odd_d = here(swap_pairs(odd_d, "depth", 1))
    own = [here(x) for x in own]
    spare_rows = (2 * depth + 2 + 7) // 8 * 8
    odd_x, even_x, *kept = pl.pallas_call(
        spare_kernel,
        out_shape=[vmem((spare_rows, width)), vmem((depth + spare_rows, width))]
        + [vmem((4, depth, width)), vmem((2, depth, width)), vmem((8, width))],
        scratch_shapes=[vmem((4, count, depth + 2 * margin, lanes))],
        compiler_params=params,
        cost_estimate=pl.CostEstimate(
            flops=40 * field.size, bytes_accessed=4 * field.size, transcendentals=0
        ),
        name="spare",
    )(*own)
    odd_x = here(swap_pairs(odd_x, "rows", 1))
    even_x = here(swap_pairs(even_x, "rows", 0))
    kept = [here(x) for x in kept]
    odd_2, even_2, middles, partly, sides = pl.pallas_call(
        edge_kernel,
        out_shape=[
            vmem((depth + 8, width)),
            vmem((depth + 8, width)),
            vmem((4, depth, width)),
            vmem((2, depth, width)),
            vmem((2, 2, rows, width)),
        ],
        scratch_shapes=[
            vmem((2, count, depth + 2 * margin, lanes)),
            vmem((count, 8 * (rows + 1), lanes)),
        ],
        compiler_params=params,
        name="edge",
    )(*own[1:], even_d, odd_d, odd_f, even_x, here(near), *kept)
    odd_2 = here(swap_pairs(odd_2, "rows", 1))
    even_2 = here(swap_pairs(even_2, "rows", 0))
    middles, partly, sides = here(middles), here(partly), here(sides)
    held = [vmem((count, (rows + 4) * block.pitch + margin, lanes))] * 2
    held += [pltpu.HBM(field.shape, field.dtype)]
    in_vmem = pl.BlockSpec(memory_space=pltpu.VMEM)
    second, third, front = pl.pallas_call(
        inner_kernel,
        out_shape=held,
        out_specs=[in_vmem] * 2 + [in_hbm],
        scratch_shapes=[
            vmem((count, (rows + 4) * block.pitch + margin, lanes)),
            vmem(field.shape),
            pltpu.SemaphoreType.DMA,
        ],
        compiler_params=params,
        cost_estimate=pl.CostEstimate(
            flops=80 * field.size, bytes_accessed=8 * field.size, transcendentals=0
        ),
        name="inner",
    )(*own, even_d, odd_d, middles, sides)
    opacity = opacity_total / (depth * groups)
    _, _, front, partial = pl.pallas_call(
        lambda *refs: rim_kernel(opacity, *refs),
        in_specs=[in_vmem] * 14 + [in_hbm],
        out_shape=held + [vmem((4, rows, width))],
        out_specs=[in_vmem] * 2 + [in_hbm, in_vmem],
        scratch_shapes=[vmem((2, depth, width)), pltpu.SemaphoreType.DMA((2,))],
        input_output_aliases={12 + i: i for i in range(3)},
        compiler_params=params,
        name="rim",
    )(
        own[0], even_d, odd_d, odd_x, even_x, odd_2, even_2, *kept[1:], middles, partly, sides,
        here(second), here(third), far(front),
    )

    position = lax.axis_index("depth")
    split = partial.reshape(4, rows, groups, width // groups)
    parts = {}
    for apart in range(groups):
        part = lax.dynamic_index_in_dim(split, position ^ apart, 2, keepdims=False)
        if apart:
            part = lax.ppermute(part, "depth", [(i, i ^ apart) for i in range(groups)])
        parts[apart] = part
    parts = jnp.stack([parts[-apart % groups] for apart in range(groups)])
    picture = None
    for s in range(groups):
        apart = position ^ s
        segment = lax.dynamic_index_in_dim(parts, -apart % groups, 0, keepdims=False)
        if picture is None:
            colors, through = segment[:3], segment[3:]
            picture = (colors, through)
        else:
            colors = colors + through * segment[:3]
            through = through * segment[3:]
    return front, jnp.concatenate([colors, through], axis=0)


def solution(mesh):
    return jax.shard_map(
        shards,
        mesh=mesh,
        in_specs=(
            P("rows", "depth", None),
            P("rows", "depth", None),
            P(None, "rows", "depth", None),
        ),
        out_specs=(P("rows", "depth", None), P(None, "rows", "depth")),
        check_vma=False,
    )
```

```python
import jax
import jax.numpy as jnp
from jax import lax
from jax.experimental import pallas as pl
from jax.experimental.pallas import tpu as pltpu
from jax.sharding import PartitionSpec as P

time_step = 0.2
growth_rate = 1.0
opacity_total = 3.0

lanes = 128
margin = 8
halves = 1
pack_gap = 4


def pairs(count, first):
    forward = [(i, i + 1) for i in range(first, count - 1, 2)]
    return forward + [(target, source) for source, target in forward]


def swap_pairs(value, axis, first):
    return lax.ppermute(value, axis, pairs(lax.axis_size(axis), first))


def stencil(u, low, high, coef):
    diff = coef[0]
    change = growth_rate * u * (1.0 - u)
    for before, after, speed in zip(low, high, coef[1:]):
        change = change + (diff + jnp.maximum(speed, 0.0)) * (before - u)
        change = change + (diff - jnp.minimum(speed, 0.0)) * (after - u)
    return u + time_step * change


def beside(chunks):
    lane = lax.broadcasted_iota(jnp.int32, chunks[0].shape, 1)
    right = [pltpu.roll(x, 1, 1) for x in chunks]
    left = [pltpu.roll(x, lanes - 1, 1) for x in chunks]
    zero = jnp.zeros_like(chunks[0])
    count = len(chunks)
    before = [jnp.where(lane == 0, right[c - 1] if c else zero, right[c]) for c in range(count)]
    after = [
        jnp.where(lane == lanes - 1, left[c + 1] if c + 1 < count else zero, left[c])
        for c in range(count)
    ]
    return before, after


def cols(c):
    start = c * lanes
    return pl.ds(start if isinstance(c, int) else pl.multiple_of(start, lanes), lanes)


def over(count, body, unroll):
    def step(i, carry):
        body(i)
        return carry

    lax.fori_loop(0, count, step, 0, unroll=unroll)


def coef_of(diff, vel, r, c):
    return [diff[r, :, cols(c)].astype(jnp.float32)] + [
        vel[i, r, :, cols(c)].astype(jnp.float32) for i in range(3)
    ]


def weight_low(diff, speed):
    return time_step * (diff + jnp.maximum(speed, 0.0))


def weight_high(diff, speed):
    return time_step * (diff - jnp.minimum(speed, 0.0))


def pack_kernel(
    field_far, diff_far, vel_far, field, diff, vel, even_d, odd_d, odd_f, near, flat, coefs, sems
):
    rows, depth, width = field.shape
    count = width // lanes
    pitch = depth + pack_gap
    depth_odd = lax.axis_index("depth") % 2 == 1
    rows_odd = lax.axis_index("rows") % 2 == 1
    parts = [(field_far, field), (diff_far, diff)]
    parts += [(vel_far.at[i], vel.at[i]) for i in range(3)]
    step = rows // halves
    loads = [
        [
            pltpu.make_async_copy(
                source.at[pl.ds(h * step, step)], target.at[pl.ds(h * step, step)], sems.at[h, i]
            )
            for i, (source, target) in enumerate(parts)
        ]
        for h in range(halves)
    ]
    for half in loads:
        for load in half:
            load.start()
    for h, half in enumerate(loads):
        for load in half:
            load.wait()
        for c in range(count):
            for r in range(h * step, (h + 1) * step):
                place = pl.ds(r * pitch, depth)
                coef = coef_of(diff, vel, r, c)
                flat[c, place, :] = field[r, :, cols(c)]
                for i in range(4):
                    coefs[i, c, place, :] = coef[i]
    for c in range(count):
        first, last = field[0, :, cols(c)], field[rows - 1, :, cols(c)]
        odd_f[:, cols(c)] = jnp.where(rows_odd, last, first)

    row = lax.broadcasted_iota(jnp.int32, (rows, lanes), 0)
    sides = []
    for k, start, step in ((0, 0, 1), (1, depth - 1, -1)):

        def slab(ref, d):
            return [ref[c, pl.ds(d, rows, stride=pitch), :] for c in range(count)]

        u0, u1, u2 = (slab(flat, start + step * j) for j in range(3))
        near_coef = [slab(coefs.at[i], start) for i in range(4)]
        next_coef = [slab(coefs.at[i], start + step) for i in range(4)]
        before, after = beside(u1)
        side = []
        for c in range(count):
            near[k, :, cols(c)] = u0[c]
            above, below = past_rows(u1[c], row)
            deep = (u0[c], u2[c]) if step > 0 else (u2[c], u0[c])
            coef = [next_coef[i][c] for i in range(4)]
            middle = stencil(
                u1[c], (above, deep[0], before[c]), (below, deep[1], after[c]), coef
            )
            weight = row_weight(row, coef)
            side.append([u0[c], u1[c]] + [near_coef[i][c] for i in range(4)] + [middle, weight])
        sides.append(side)
    low, high = sides
    for c in range(count):
        for i in range(8):
            even_d[i, :, cols(c)] = jnp.where(depth_odd, low[c][i], high[c][i])
            odd_d[i, :, cols(c)] = jnp.where(depth_odd, high[c][i], low[c][i])


def spare_kernel(field, diff, vel, odd_x, even_x, partial, own_w, own_d, ext):
    rows, depth, width = field.shape
    every = range(width // lanes)
    rows_odd = lax.axis_index("rows") % 2 == 1
    own = pl.ds(margin, depth)
    shallow, deep = pl.ds(margin - 1, depth), pl.ds(margin + 1, depth)
    none = jnp.zeros((depth, lanes), jnp.float32)
    zero = jnp.zeros((1, lanes), jnp.float32)
    for j, r in enumerate((0, 1, rows - 2, rows - 1)):
        u = [field[r, :, cols(c)] for c in every]
        before, after = beside(u)
        for c in every:
            ext[j, c, margin - 1 : margin, :] = zero
            ext[j, c, own, :] = u[c]
            ext[j, c, margin + depth : margin + depth + 1, :] = zero
        for c in every:
            above = field[r - 1, :, cols(c)] if r > 0 else none
            below = field[r + 1, :, cols(c)] if r < rows - 1 else none
            coef = coef_of(diff, vel, r, c)
            partial[j, :, cols(c)] = stencil(
                u[c],
                (above, ext[j, c, shallow, :], before[c]),
                (below, ext[j, c, deep, :], after[c]),
                coef,
            )
            low = weight_low(coef[0], coef[2])[0:1]
            high = weight_high(coef[0], coef[2])[depth - 1 : depth]
            own_d[2 * j : 2 * j + 1, cols(c)] = low
            own_d[2 * j + 1 : 2 * j + 2, cols(c)] = high
            if r == 0:
                own_w[0, :, cols(c)] = weight_low(coef[0], coef[1])
            if r == rows - 1:
                own_w[1, :, cols(c)] = weight_high(coef[0], coef[1])
    for c in every:
        first, last = field[0, :, cols(c)], field[rows - 1, :, cols(c)]
        even_x[:depth, cols(c)] = jnp.where(rows_odd, first, last)
        for start, length, low, high in (
            (0, depth, own_w[0, :, cols(c)], own_w[1, :, cols(c)]),
            (depth, depth, partial[0, :, cols(c)], partial[3, :, cols(c)]),
            (2 * depth, 2, own_d[0:2, cols(c)], own_d[6:8, cols(c)]),
        ):
            even_x[pl.ds(depth + start, length), cols(c)] = jnp.where(rows_odd, low, high)
            odd_x[pl.ds(start, length), cols(c)] = jnp.where(rows_odd, high, low)


def arrived(even, odd, is_odd, index, even_index=None):
    a, b = even[index if even_index is None else even_index], odd[index]
    return jnp.where(is_odd, a, b), jnp.where(is_odd, b, a)


def past_rows(u, row):
    rows = u.shape[0]
    above = jnp.where(row == 0, 0.0, pltpu.roll(u, 1, 0))
    below = jnp.where(row == rows - 1, 0.0, pltpu.roll(u, rows - 1, 0))
    return above, below


def row_weight(row, coef):
    return jnp.where(row == 0, weight_low(coef[0], coef[1]), weight_high(coef[0], coef[1]))


def at_ends(first, last, shape):
    place = lax.broadcasted_iota(jnp.int32, shape, 0)
    return jnp.where(place == 0, first, jnp.where(place == shape[0] - 1, last, 0.0))


def edge_kernel(
    diff, vel, even_d, odd_d, odd_f, even_x, near, partial, own_w, own_d,
    odd_2, even_2, middles, partly, sides, ext, stack,
):
    _, rows, width = even_d.shape
    depth = diff.shape[1]
    every = range(width // lanes)
    depth_odd = lax.axis_index("depth") % 2 == 1
    rows_odd = lax.axis_index("rows") % 2 == 1
    own = pl.ds(margin, depth)
    shallow, deep = pl.ds(margin - 1, depth), pl.ds(margin + 1, depth)
    row = lax.broadcasted_iota(jnp.int32, (rows, lanes), 0)
    none = jnp.zeros((depth, lanes), jnp.float32)
    zero = jnp.zeros((1, lanes), jnp.float32)
    lines = {j: [] for j in range(4)}
    for c in every:
        beyond = arrived(even_x, odd_f, rows_odd, (pl.ds(0, depth), cols(c)))
        for j, r in enumerate((0, 1, rows - 2, rows - 1)):
            value = partial[j, :, cols(c)]
            if j in (0, 3):
                value = value + own_w[j // 3, :, cols(c)] * beyond[j // 3]
            both = arrived(even_d, odd_d, depth_odd, (0, pl.ds(r, 1), cols(c)))
            weights = [own_d[2 * j + k : 2 * j + k + 1, cols(c)] for k in range(2)]
            value = value + at_ends(weights[0] * both[0], weights[1] * both[1], value.shape)
            lines[j].append(value)
            middles[j, :, cols(c)] = value
            if j in (0, 3):
                ext[j // 3, c, margin - 1 : margin, :] = zero
                ext[j // 3, c, own, :] = value
                ext[j // 3, c, margin + depth : margin + depth + 1, :] = zero
    for j, inner, r in ((0, 1, 0), (3, 2, rows - 1)):
        u = lines[j]
        before, after = beside(u)
        for c in every:
            next_row = lines[inner][c]
            above, below = (none, next_row) if r == 0 else (next_row, none)
            partly[j // 3, :, cols(c)] = stencil(
                u[c],
                (above, ext[j // 3, c, shallow, :], before[c]),
                (below, ext[j // 3, c, deep, :], after[c]),
                coef_of(diff, vel, r, c),
            )
    for c in every:
        first, last = partly[0, :, cols(c)], partly[1, :, cols(c)]
        even_2[:depth, cols(c)] = jnp.where(rows_odd, first, last)
        odd_2[:depth, cols(c)] = jnp.where(rows_odd, last, first)

    def came(item, c, k):
        return arrived(even_d, odd_d, depth_odd, (item, slice(None), cols(c)))[k]

    for k in range(2):
        u = [came(0, c, k) for c in every]
        before, after = beside(u)
        for c in every:
            above, below = past_rows(u[c], row)
            here_d, beyond_d = near[k, :, cols(c)], came(1, c, k)
            low_d, high_d = (beyond_d, here_d) if k == 0 else (here_d, beyond_d)
            coef = [came(2 + i, c, k) for i in range(4)]
            sides[k, 0, :, cols(c)] = stencil(
                u[c], (above, low_d, before[c]), (below, high_d, after[c]), coef
            )
            sides[k, 1, :, cols(c)] = row_weight(row, coef)
            values = (u[c], beyond_d, sides[k, 0, :, cols(c)], sides[k, 1, :, cols(c)])
            for j, value in enumerate(values):
                stack[c, pl.ds((4 * k + j) * (rows + 1), rows), :] = value
    for c in every:
        first = stack[c, pl.ds(0, 8, stride=rows + 1), :]
        last = stack[c, pl.ds(rows - 1, 8, stride=rows + 1), :]
        even_2[depth : depth + 8, cols(c)] = jnp.where(rows_odd, first, last)
        odd_2[depth : depth + 8, cols(c)] = jnp.where(rows_odd, last, first)


class Block:
    def __init__(self, rows, depth, width):
        self.rows, self.depth, self.every = rows, depth, range(width // lanes)
        self.pitch = depth + 2 * margin + 1

    def at(self, r, d):
        return (r + 2) * self.pitch + margin + d

    def along(self, r, d=0):
        return pl.ds(self.at(r, d), self.depth)

    def across(self, r, d, length):
        return pl.ds(self.at(r, d), length, stride=self.pitch)

    def line(self, ref, r, d=0):
        return [ref[c, self.along(r, d), :] for c in self.every]

    def slab(self, ref, r, d, length):
        return [ref[c, self.across(r, d, length), :] for c in self.every]

    def put(self, ref, place, values):
        for c in self.every:
            ref[c, place, :] = values[c]

    def section_line(self, ref, r, coef):
        u = self.line(ref, r)
        before, after = beside(u)
        low = (self.line(ref, r - 1), self.line(ref, r, -1), before)
        high = (self.line(ref, r + 1), self.line(ref, r, 1), after)
        return [
            stencil(u[c], [x[c] for x in low], [x[c] for x in high], coef(c)) for c in self.every
        ]

    def section_slab(self, ref, r, d, length, coef):
        u = self.slab(ref, r, d, length)
        before, after = beside(u)
        low = (self.slab(ref, r - 1, d, length), self.slab(ref, r, d - 1, length), before)
        high = (self.slab(ref, r + 1, d, length), self.slab(ref, r, d + 1, length), after)
        return [
            stencil(u[c], [x[c] for x in low], [x[c] for x in high], coef(c)) for c in self.every
        ]


def inner_kernel(
    field, diff, vel, even_d, odd_d, middles, sides,
    second, third, front_far, first, front, sem,
):
    rows, depth, width = field.shape
    block = Block(rows, depth, width)
    depth_odd = lax.axis_index("depth") % 2 == 1
    for c in block.every:
        for r in range(1, rows - 1):
            first[c, block.along(r), :] = field[r, :, cols(c)]
        low, high = arrived(even_d, odd_d, depth_odd, (0, slice(None), cols(c)))
        first[c, block.across(0, -1, rows), :] = low
        first[c, block.across(0, depth, rows), :] = high
        low, high = arrived(even_d, odd_d, depth_odd, (6, slice(None), cols(c)))
        second[c, block.across(0, -2, rows), :] = low
        second[c, block.across(0, depth + 1, rows), :] = high
        second[c, block.across(0, -1, rows), :] = sides[0, 0, :, cols(c)]
        second[c, block.across(0, depth, rows), :] = sides[1, 0, :, cols(c)]
        for j, r in enumerate((0, 1, rows - 2, rows - 1)):
            second[c, block.along(r), :] = middles[j, :, cols(c)]

    def own_middle(r, carry):
        values = block.section_line(first, r, lambda c: coef_of(diff, vel, r, c))
        block.put(second, block.along(r), values)
        return carry

    lax.fori_loop(2, rows - 2, own_middle, 0)

    def own_front(r, carry):
        values = block.section_line(second, r, lambda c: coef_of(diff, vel, r, c))
        block.put(third, block.along(r), values)
        for c in block.every:
            front[r, :, cols(c)] = values[c]
        return carry

    lax.fori_loop(1, rows - 1, own_front, 0)
    within = pl.ds(1, rows - 2)
    save = pltpu.make_async_copy(front.at[within], front_far.at[within], sem)
    save.start()
    save.wait()


def rim_kernel(
    opacity, field, even_d, odd_d, odd_x, even_x, odd_2, even_2, own_w, own_d, middles, partly, sides,
    *refs
):
    second, third, front_far, partial, front, sems = refs[3:]
    rows, depth, width = field.shape
    block = Block(rows, depth, width)
    every = block.every
    depth_odd = lax.axis_index("depth") % 2 == 1
    rows_odd = lax.axis_index("rows") % 2 == 1
    line = (depth, lanes)

    def spare(start, length, c):
        index = (slice(start, start + length), cols(c))
        shifted = (slice(depth + start, depth + start + length), cols(c))
        return arrived(even_x, odd_x, rows_odd, index, shifted)

    def corner(k, j, c):
        place = depth + 4 * k + j
        return arrived(even_2, odd_2, rows_odd, (slice(place, place + 1), cols(c)))

    def cell(ref, c, r, d, value):
        ref[c, pl.ds(block.at(r, d), 1), :] = value

    ends = ((0, 0, -1), (1, depth - 1, depth))
    rims = ((0, 0, -1), (1, rows - 1, rows))

    def around(c):
        weights, parts = spare(0, depth, c), spare(depth, depth, c)
        fronts = arrived(even_2, odd_2, rows_odd, (slice(0, depth), cols(c)))
        along = [spare(2 * depth + k, 1, c) for k in range(2)]
        corners = [[corner(k, j, c) for j in range(4)] for k in range(2)]
        for e, r, past in rims:
            near = [corners[k][0][e] for k in range(2)]
            middle = parts[e] + weights[e] * field[r, :, cols(c)]
            middle = middle + at_ends(along[0][e] * near[0], along[1][e] * near[1], line)
            second[c, block.along(past), :] = middle
            own_ends, past_ends = [], []
            for k, d, beyond in ends:
                index = (slice(r, r + 1), cols(c))
                outside = arrived(even_d, odd_d, depth_odd, (0, *index))[k]
                next_cell = arrived(even_d, odd_d, depth_odd, (6, *index))[k]
                next_weight = arrived(even_d, odd_d, depth_odd, (7, *index))[k]
                _, far_cell, part, weight = (x[e] for x in corners[k])
                past_ends.append(part + weight * outside)
                own_ends.append(sides[k, 0, *index] + sides[k, 1, *index] * near[k])
                cell(second, c, past, beyond, past_ends[k])
                cell(second, c, r, beyond, own_ends[k])
                cell(second, c, r, 2 * beyond - d, next_cell + next_weight * far_cell)
            own_along = [own_d[6 * e + k : 6 * e + k + 1, cols(c)] for k in range(2)]
            value = partly[e, :, cols(c)] + own_w[e, :, cols(c)] * middle
            value = value + at_ends(
                own_along[0] * own_ends[0], own_along[1] * own_ends[1], line
            )
            third[c, block.along(r), :] = value
            front[e, :, cols(c)] = value
            value = fronts[e] + weights[e] * middles[3 * e, :, cols(c)]
            third[c, block.along(past), :] = value + at_ends(
                along[0][e] * past_ends[0], along[1][e] * past_ends[1], line
            )

    over(len(every), around, 2)
    saves = [
        pltpu.make_async_copy(front.at[e], front_far.at[r], sems.at[e]) for e, r, past in rims
    ]
    for save in saves:
        save.start()
    for k, d, beyond in ends:
        items = [
            [
                arrived(even_d, odd_d, depth_odd, (2 + i, slice(None), cols(c)))[k]
                for i in range(4)
            ]
            for c in every
        ]
        values = block.section_slab(second, 0, beyond, rows, lambda c: items[c])
        block.put(third, block.across(0, beyond, rows), values)

    def shine(d, carry):
        shallow, center, deep = (block.slab(third, 0, d + i, rows) for i in (-1, 0, 1))
        before, after = beside(center)
        above, below = block.slab(third, -1, d, rows), block.slab(third, 1, d, rows)
        result = []
        for c in every:
            through, total, red, green = carry[c]
            u = center[c]
            grad_row = below[c] - above[c]
            grad_deep = deep[c] - shallow[c]
            grad_col = after[c] - before[c]
            lighting = 0.48 * grad_row + 0.64 * grad_deep + 0.6 * grad_col
            magnitude = grad_row * grad_row + grad_deep * grad_deep + grad_col * grad_col + 0.4
            shade = 0.35 + 0.65 * lighting * lighting / magnitude
            passed = jnp.exp(-opacity * u)
            weight = through * (1.0 - passed) * shade
            colored = weight * u
            result.append((through * passed, total + weight, red + colored, green + colored * u))
        return tuple(result)

    zero, one = jnp.zeros((rows, lanes), jnp.float32), jnp.ones((rows, lanes), jnp.float32)
    carry = tuple((one, zero, zero, zero) for _ in every)
    carry = lax.fori_loop(0, depth, shine, carry, unroll=8)
    for c, (through, total, red, green) in enumerate(carry):
        partial[0, :, cols(c)] = red
        partial[1, :, cols(c)] = green
        partial[2, :, cols(c)] = total - red
        partial[3, :, cols(c)] = through
    for save in saves:
        save.wait()


def vmem(shape):
    return pltpu.VMEM(shape, jnp.float32)


def here(value):
    return pltpu.with_memory_space_constraint(value, pltpu.VMEM)


def far(value):
    return pltpu.with_memory_space_constraint(value, pltpu.HBM)


def shards(field, diffusivity, velocity):
    rows, depth, width = field.shape
    count = width // lanes
    block = Block(rows, depth, width)
    groups = lax.axis_size("depth")
    params = pltpu.CompilerParams(vmem_limit_bytes=24 * 2**20)
    in_hbm = pl.BlockSpec(memory_space=pltpu.HBM)

    own_types = [pltpu.VMEM(x.shape, x.dtype) for x in (field, diffusivity, velocity)]
    *own, even_d, odd_d, odd_f, near = pl.pallas_call(
        pack_kernel,
        in_specs=[in_hbm] * 3,
        out_shape=own_types
        + [vmem((8, rows, width))] * 2
        + [vmem((depth, width)), vmem((2, rows, width))],
        scratch_shapes=[
            vmem((count, rows * (depth + pack_gap), lanes)),
            vmem((4, count, rows * (depth + pack_gap), lanes)),
            pltpu.SemaphoreType.DMA((halves, 5)),
        ],
        compiler_params=params,
        name="pack",
    )(far(field), far(diffusivity), far(velocity))
    odd_f = here(swap_pairs(odd_f, "rows", 1))
    even_d = here(swap_pairs(even_d, "depth", 0))
    odd_d = here(swap_pairs(odd_d, "depth", 1))
    own = [here(x) for x in own]
    spare_rows = (2 * depth + 2 + 7) // 8 * 8
    odd_x, even_x, *kept = pl.pallas_call(
        spare_kernel,
        out_shape=[vmem((spare_rows, width)), vmem((depth + spare_rows, width))]
        + [vmem((4, depth, width)), vmem((2, depth, width)), vmem((8, width))],
        scratch_shapes=[vmem((4, count, depth + 2 * margin, lanes))],
        compiler_params=params,
        cost_estimate=pl.CostEstimate(
            flops=40 * field.size, bytes_accessed=4 * field.size, transcendentals=0
        ),
        name="spare",
    )(*own)
    odd_x = here(swap_pairs(odd_x, "rows", 1))
    even_x = here(swap_pairs(even_x, "rows", 0))
    kept = [here(x) for x in kept]
    odd_2, even_2, middles, partly, sides = pl.pallas_call(
        edge_kernel,
        out_shape=[
            vmem((depth + 8, width)),
            vmem((depth + 8, width)),
            vmem((4, depth, width)),
            vmem((2, depth, width)),
            vmem((2, 2, rows, width)),
        ],
        scratch_shapes=[
            vmem((2, count, depth + 2 * margin, lanes)),
            vmem((count, 8 * (rows + 1), lanes)),
        ],
        compiler_params=params,
        name="edge",
    )(*own[1:], even_d, odd_d, odd_f, even_x, here(near), *kept)
    odd_2 = here(swap_pairs(odd_2, "rows", 1))
    even_2 = here(swap_pairs(even_2, "rows", 0))
    middles, partly, sides = here(middles), here(partly), here(sides)
    held = [vmem((count, (rows + 4) * block.pitch + margin, lanes))] * 2
    held += [pltpu.HBM(field.shape, field.dtype)]
    in_vmem = pl.BlockSpec(memory_space=pltpu.VMEM)
    second, third, front = pl.pallas_call(
        inner_kernel,
        out_shape=held,
        out_specs=[in_vmem] * 2 + [in_hbm],
        scratch_shapes=[
            vmem((count, (rows + 4) * block.pitch + margin, lanes)),
            vmem(field.shape),
            pltpu.SemaphoreType.DMA,
        ],
        compiler_params=params,
        cost_estimate=pl.CostEstimate(
            flops=80 * field.size, bytes_accessed=8 * field.size, transcendentals=0
        ),
        name="inner",
    )(*own, even_d, odd_d, middles, sides)
    opacity = opacity_total / (depth * groups)
    _, _, front, partial = pl.pallas_call(
        lambda *refs: rim_kernel(opacity, *refs),
        in_specs=[in_vmem] * 14 + [in_hbm],
        out_shape=held + [vmem((4, rows, width))],
        out_specs=[in_vmem] * 2 + [in_hbm, in_vmem],
        scratch_shapes=[vmem((2, depth, width)), pltpu.SemaphoreType.DMA((2,))],
        input_output_aliases={12 + i: i for i in range(3)},
        compiler_params=params,
        name="rim",
    )(
        own[0], even_d, odd_d, odd_x, even_x, odd_2, even_2, *kept[1:], middles, partly, sides,
        here(second), here(third), far(front),
    )

    position = lax.axis_index("depth")
    split = partial.reshape(4, rows, groups, width // groups)
    parts = {}
    for apart in range(groups):
        part = lax.dynamic_index_in_dim(split, position ^ apart, 2, keepdims=False)
        if apart:
            part = lax.ppermute(part, "depth", [(i, i ^ apart) for i in range(groups)])
        parts[apart] = part
    parts = jnp.stack([parts[-apart % groups] for apart in range(groups)])
    picture = None
    for s in range(groups):
        apart = position ^ s
        segment = lax.dynamic_index_in_dim(parts, -apart % groups, 0, keepdims=False)
        if picture is None:
            colors, through = segment[:3], segment[3:]
            picture = (colors, through)
        else:
            colors = colors + through * segment[:3]
            through = through * segment[3:]
    return front, jnp.concatenate([colors, through], axis=0)


def solution(mesh):
    return jax.shard_map(
        shards,
        mesh=mesh,
        in_specs=(
            P("rows", "depth", None),
            P("rows", "depth", None),
            P(None, "rows", "depth", None),
        ),
        out_specs=(P("rows", "depth", None), P(None, "rows", "depth")),
        check_vma=False,
    )
```

```python
import jax
import jax.numpy as jnp
from jax import lax
from jax.experimental import pallas as pl
from jax.experimental.pallas import tpu as pltpu
from jax.sharding import PartitionSpec as P

time_step = 0.2
growth_rate = 1.0
opacity_total = 3.0

lanes = 128
margin = 8
halves = 1
pack_gap = 4


def pairs(count, first):
    forward = [(i, i + 1) for i in range(first, count - 1, 2)]
    return forward + [(target, source) for source, target in forward]


def swap_pairs(value, axis, first):
    return lax.ppermute(value, axis, pairs(lax.axis_size(axis), first))


def stencil(u, low, high, coef):
    diff = coef[0]
    change = growth_rate * u * (1.0 - u)
    for before, after, speed in zip(low, high, coef[1:]):
        change = change + (diff + jnp.maximum(speed, 0.0)) * (before - u)
        change = change + (diff - jnp.minimum(speed, 0.0)) * (after - u)
    return u + time_step * change


def beside(chunks):
    lane = lax.broadcasted_iota(jnp.int32, chunks[0].shape, 1)
    right = [pltpu.roll(x, 1, 1) for x in chunks]
    left = [pltpu.roll(x, lanes - 1, 1) for x in chunks]
    zero = jnp.zeros_like(chunks[0])
    count = len(chunks)
    before = [jnp.where(lane == 0, right[c - 1] if c else zero, right[c]) for c in range(count)]
    after = [
        jnp.where(lane == lanes - 1, left[c + 1] if c + 1 < count else zero, left[c])
        for c in range(count)
    ]
    return before, after


def cols(c):
    start = c * lanes
    return pl.ds(start if isinstance(c, int) else pl.multiple_of(start, lanes), lanes)


def over(count, body, unroll):
    def step(i, carry):
        body(i)
        return carry

    lax.fori_loop(0, count, step, 0, unroll=unroll)


def coef_of(diff, vel, r, c):
    return [diff[r, :, cols(c)].astype(jnp.float32)] + [
        vel[i, r, :, cols(c)].astype(jnp.float32) for i in range(3)
    ]


def weight_low(diff, speed):
    return time_step * (diff + jnp.maximum(speed, 0.0))


def weight_high(diff, speed):
    return time_step * (diff - jnp.minimum(speed, 0.0))


def pack_kernel(
    field_far, diff_far, vel_far, field, diff, vel, even_d, odd_d, odd_f, near, flat, coefs, sems
):
    rows, depth, width = field.shape
    count = width // lanes
    pitch = depth + pack_gap
    depth_odd = lax.axis_index("depth") % 2 == 1
    rows_odd = lax.axis_index("rows") % 2 == 1
    parts = [(field_far, field), (diff_far, diff)]
    parts += [(vel_far.at[i], vel.at[i]) for i in range(3)]
    step = rows // halves
    loads = [
        [
            pltpu.make_async_copy(
                source.at[pl.ds(h * step, step)], target.at[pl.ds(h * step, step)], sems.at[h, i]
            )
            for i, (source, target) in enumerate(parts)
        ]
        for h in range(halves)
    ]
    for half in loads:
        for load in half:
            load.start()
    for h, half in enumerate(loads):
        for load in half:
            load.wait()
        for c in range(count):
            for r in range(h * step, (h + 1) * step):
                place = pl.ds(r * pitch, depth)
                coef = coef_of(diff, vel, r, c)
                flat[c, place, :] = field[r, :, cols(c)]
                for i in range(4):
                    coefs[i, c, place, :] = coef[i]
    for c in range(count):
        first, last = field[0, :, cols(c)], field[rows - 1, :, cols(c)]
        odd_f[:, cols(c)] = jnp.where(rows_odd, last, first)

    row = lax.broadcasted_iota(jnp.int32, (rows, lanes), 0)
    sides = []
    for k, start, step in ((0, 0, 1), (1, depth - 1, -1)):

        def slab(ref, d):
            return [ref[c, pl.ds(d, rows, stride=pitch), :] for c in range(count)]

        u0, u1, u2 = (slab(flat, start + step * j) for j in range(3))
        near_coef = [slab(coefs.at[i], start) for i in range(4)]
        next_coef = [slab(coefs.at[i], start + step) for i in range(4)]
        before, after = beside(u1)
        side = []
        for c in range(count):
            near[k, :, cols(c)] = u0[c]
            above, below = past_rows(u1[c], row)
            deep = (u0[c], u2[c]) if step > 0 else (u2[c], u0[c])
            coef = [next_coef[i][c] for i in range(4)]
            middle = stencil(
                u1[c], (above, deep[0], before[c]), (below, deep[1], after[c]), coef
            )
            weight = row_weight(row, coef)
            side.append([u0[c], u1[c]] + [near_coef[i][c] for i in range(4)] + [middle, weight])
        sides.append(side)
    low, high = sides
    for c in range(count):
        for i in range(7):
            even_d[of_deep(rows, c, i)] = jnp.where(depth_odd, low[c][i], high[c][i])
            odd_d[of_deep(rows, c, i)] = jnp.where(depth_odd, high[c][i], low[c][i])
        for i, r in enumerate((0, rows - 1)):
            f_val, l_val = low[c][7][r : r + 1], high[c][7][r : r + 1]
            even_d[of_deep(rows, c, 7, i, 1)] = jnp.where(depth_odd, f_val, l_val)
            odd_d[of_deep(rows, c, 7, i, 1)] = jnp.where(depth_odd, l_val, f_val)


def spare_kernel(field, diff, vel, odd_x, even_x, partial, own_w, own_d, ext):
    rows, depth, width = field.shape
    every = range(width // lanes)
    rows_odd = lax.axis_index("rows") % 2 == 1
    own = pl.ds(margin, depth)
    shallow, deep = pl.ds(margin - 1, depth), pl.ds(margin + 1, depth)
    none = jnp.zeros((depth, lanes), jnp.float32)
    zero = jnp.zeros((1, lanes), jnp.float32)
    for j, r in enumerate((0, 1, rows - 2, rows - 1)):
        u = [field[r, :, cols(c)] for c in every]
        before, after = beside(u)
        for c in every:
            ext[j, c, margin - 1 : margin, :] = zero
            ext[j, c, own, :] = u[c]
            ext[j, c, margin + depth : margin + depth + 1, :] = zero
        for c in every:
            above = field[r - 1, :, cols(c)] if r > 0 else none
            below = field[r + 1, :, cols(c)] if r < rows - 1 else none
            coef = coef_of(diff, vel, r, c)
            partial[j, :, cols(c)] = stencil(
                u[c],
                (above, ext[j, c, shallow, :], before[c]),
                (below, ext[j, c, deep, :], after[c]),
                coef,
            )
            low = weight_low(coef[0], coef[2])[0:1]
            high = weight_high(coef[0], coef[2])[depth - 1 : depth]
            own_d[2 * j : 2 * j + 1, cols(c)] = low
            own_d[2 * j + 1 : 2 * j + 2, cols(c)] = high
            if r == 0:
                own_w[0, :, cols(c)] = weight_low(coef[0], coef[1])
            if r == rows - 1:
                own_w[1, :, cols(c)] = weight_high(coef[0], coef[1])
    for c in every:
        first, last = field[0, :, cols(c)], field[rows - 1, :, cols(c)]
        even_x[:depth, cols(c)] = jnp.where(rows_odd, first, last)
        for start, length, low, high in (
            (0, depth, own_w[0, :, cols(c)], own_w[1, :, cols(c)]),
            (depth, depth, partial[0, :, cols(c)], partial[3, :, cols(c)]),
            (2 * depth, 2, own_d[0:2, cols(c)], own_d[6:8, cols(c)]),
        ):
            even_x[pl.ds(depth + start, length), cols(c)] = jnp.where(rows_odd, low, high)
            odd_x[pl.ds(start, length), cols(c)] = jnp.where(rows_odd, high, low)


def arrived(even, odd, is_odd, index, even_index=None):
    a, b = even[index if even_index is None else even_index], odd[index]
    return jnp.where(is_odd, a, b), jnp.where(is_odd, b, a)


def deep_rows(rows):
    return 7 * rows + 2


def of_deep(rows, c, item, start=0, length=None):
    place = c * deep_rows(rows) + item * rows + start
    return pl.ds(place, rows if length is None else length), slice(None)


def past_rows(u, row):
    rows = u.shape[0]
    above = jnp.where(row == 0, 0.0, pltpu.roll(u, 1, 0))
    below = jnp.where(row == rows - 1, 0.0, pltpu.roll(u, rows - 1, 0))
    return above, below


def row_weight(row, coef):
    return jnp.where(row == 0, weight_low(coef[0], coef[1]), weight_high(coef[0], coef[1]))


def at_ends(first, last, shape):
    place = lax.broadcasted_iota(jnp.int32, shape, 0)
    return jnp.where(place == 0, first, jnp.where(place == shape[0] - 1, last, 0.0))


def edge_kernel(
    diff, vel, even_d, odd_d, odd_f, even_x, near, partial, own_w, own_d,
    odd_2, even_2, middles, partly, sides, ext, stack,
):
    _, rows, width = near.shape
    depth = diff.shape[1]
    every = range(width // lanes)
    depth_odd = lax.axis_index("depth") % 2 == 1
    rows_odd = lax.axis_index("rows") % 2 == 1
    own = pl.ds(margin, depth)
    shallow, deep = pl.ds(margin - 1, depth), pl.ds(margin + 1, depth)
    row = lax.broadcasted_iota(jnp.int32, (rows, lanes), 0)
    none = jnp.zeros((depth, lanes), jnp.float32)
    zero = jnp.zeros((1, lanes), jnp.float32)
    lines = {j: [] for j in range(4)}
    for c in every:
        beyond = arrived(even_x, odd_f, rows_odd, (pl.ds(0, depth), cols(c)))
        for j, r in enumerate((0, 1, rows - 2, rows - 1)):
            value = partial[j, :, cols(c)]
            if j in (0, 3):
                value = value + own_w[j // 3, :, cols(c)] * beyond[j // 3]
            both = arrived(even_d, odd_d, depth_odd, of_deep(rows, c, 0, r, 1))
            weights = [own_d[2 * j + k : 2 * j + k + 1, cols(c)] for k in range(2)]
            value = value + at_ends(weights[0] * both[0], weights[1] * both[1], value.shape)
            lines[j].append(value)
            middles[j, :, cols(c)] = value
            if j in (0, 3):
                ext[j // 3, c, margin - 1 : margin, :] = zero
                ext[j // 3, c, own, :] = value
                ext[j // 3, c, margin + depth : margin + depth + 1, :] = zero
    for j, inner, r in ((0, 1, 0), (3, 2, rows - 1)):
        u = lines[j]
        before, after = beside(u)
        for c in every:
            next_row = lines[inner][c]
            above, below = (none, next_row) if r == 0 else (next_row, none)
            partly[j // 3, :, cols(c)] = stencil(
                u[c],
                (above, ext[j // 3, c, shallow, :], before[c]),
                (below, ext[j // 3, c, deep, :], after[c]),
                coef_of(diff, vel, r, c),
            )
    for c in every:
        first, last = partly[0, :, cols(c)], partly[1, :, cols(c)]
        even_2[:depth, cols(c)] = jnp.where(rows_odd, first, last)
        odd_2[:depth, cols(c)] = jnp.where(rows_odd, last, first)

    def came(item, c, k):
        return arrived(even_d, odd_d, depth_odd, of_deep(rows, c, item))[k]

    for k in range(2):
        u = [came(0, c, k) for c in every]
        before, after = beside(u)
        for c in every:
            above, below = past_rows(u[c], row)
            here_d, beyond_d = near[k, :, cols(c)], came(1, c, k)
            low_d, high_d = (beyond_d, here_d) if k == 0 else (here_d, beyond_d)
            coef = [came(2 + i, c, k) for i in range(4)]
            sides[k, 0, :, cols(c)] = stencil(
                u[c], (above, low_d, before[c]), (below, high_d, after[c]), coef
            )
            sides[k, 1, :, cols(c)] = row_weight(row, coef)
            values = (u[c], beyond_d, sides[k, 0, :, cols(c)], sides[k, 1, :, cols(c)])
            for j, value in enumerate(values):
                stack[c, pl.ds((4 * k + j) * (rows + 1), rows), :] = value
    for c in every:
        first = stack[c, pl.ds(0, 8, stride=rows + 1), :]
        last = stack[c, pl.ds(rows - 1, 8, stride=rows + 1), :]
        even_2[depth : depth + 8, cols(c)] = jnp.where(rows_odd, first, last)
        odd_2[depth : depth + 8, cols(c)] = jnp.where(rows_odd, last, first)


class Block:
    def __init__(self, rows, depth, width):
        self.rows, self.depth, self.every = rows, depth, range(width // lanes)
        self.pitch = depth + margin + 1

    def at(self, r, d):
        return (r + 1) * self.pitch + margin + d

    def along(self, r, d=0):
        return pl.ds(self.at(r, d), self.depth)

    def across(self, r, d, length):
        return pl.ds(self.at(r, d), length, stride=self.pitch)

    def line(self, ref, r, d=0):
        return [ref[c, self.along(r, d), :] for c in self.every]

    def slab(self, ref, r, d, length):
        return [ref[c, self.across(r, d, length), :] for c in self.every]

    def put(self, ref, place, values):
        for c in self.every:
            ref[c, place, :] = values[c]

    def section_line(self, ref, r, coef):
        u = self.line(ref, r)
        before, after = beside(u)
        low = (self.line(ref, r - 1), self.line(ref, r, -1), before)
        high = (self.line(ref, r + 1), self.line(ref, r, 1), after)
        return [
            stencil(u[c], [x[c] for x in low], [x[c] for x in high], coef(c)) for c in self.every
        ]

    def section_slab(self, ref, r, d, length, coef):
        u = self.slab(ref, r, d, length)
        before, after = beside(u)
        low = (self.slab(ref, r - 1, d, length), self.slab(ref, r, d - 1, length), before)
        high = (self.slab(ref, r + 1, d, length), self.slab(ref, r, d + 1, length), after)
        return [
            stencil(u[c], [x[c] for x in low], [x[c] for x in high], coef(c)) for c in self.every
        ]


def inner_kernel(
    field, diff, vel, even_d, odd_d, middles, sides,
    second, third, front_far, first, front, sem,
):
    rows, depth, width = field.shape
    block = Block(rows, depth, width)
    depth_odd = lax.axis_index("depth") % 2 == 1
    for c in block.every:
        for r in range(1, rows - 1):
            first[c, block.along(r), :] = field[r, :, cols(c)]
        low, high = arrived(even_d, odd_d, depth_odd, of_deep(rows, c, 0))
        first[c, block.across(0, -1, rows), :] = low
        first[c, block.across(0, depth, rows), :] = high
        low, high = arrived(even_d, odd_d, depth_odd, of_deep(rows, c, 6))
        second[c, block.across(0, -2, rows), :] = low
        second[c, block.across(0, depth + 1, rows), :] = high
        second[c, block.across(0, -1, rows), :] = sides[0, 0, :, cols(c)]
        second[c, block.across(0, depth, rows), :] = sides[1, 0, :, cols(c)]
        for j, r in enumerate((0, 1, rows - 2, rows - 1)):
            second[c, block.along(r), :] = middles[j, :, cols(c)]

    def own_middle(r, carry):
        values = block.section_line(first, r, lambda c: coef_of(diff, vel, r, c))
        block.put(second, block.along(r), values)
        return carry

    lax.fori_loop(2, rows - 2, own_middle, 0)

    def own_front(r, carry):
        values = block.section_line(second, r, lambda c: coef_of(diff, vel, r, c))
        block.put(third, block.along(r), values)
        for c in block.every:
            front[r, :, cols(c)] = values[c]
        return carry

    lax.fori_loop(1, rows - 1, own_front, 0)
    within = pl.ds(1, rows - 2)
    save = pltpu.make_async_copy(front.at[within], front_far.at[within], sem)
    save.start()
    save.wait()


def rim_kernel(
    opacity, field, even_d, odd_d, odd_x, even_x, odd_2, even_2, own_w, own_d, middles, partly, sides,
    *refs
):
    second, third, front_far, partial, front, sems = refs[3:]
    rows, depth, width = field.shape
    block = Block(rows, depth, width)
    every = block.every
    depth_odd = lax.axis_index("depth") % 2 == 1
    rows_odd = lax.axis_index("rows") % 2 == 1
    line = (depth, lanes)

    def spare(start, length, c):
        index = (slice(start, start + length), cols(c))
        shifted = (slice(depth + start, depth + start + length), cols(c))
        return arrived(even_x, odd_x, rows_odd, index, shifted)

    def corner(k, j, c):
        place = depth + 4 * k + j
        return arrived(even_2, odd_2, rows_odd, (slice(place, place + 1), cols(c)))

    def cell(ref, c, r, d, value):
        ref[c, pl.ds(block.at(r, d), 1), :] = value

    ends = ((0, 0, -1), (1, depth - 1, depth))
    rims = ((0, 0, -1), (1, rows - 1, rows))

    def around(c):
        weights, parts = spare(0, depth, c), spare(depth, depth, c)
        fronts = arrived(even_2, odd_2, rows_odd, (slice(0, depth), cols(c)))
        along = [spare(2 * depth + k, 1, c) for k in range(2)]
        corners = [[corner(k, j, c) for j in range(4)] for k in range(2)]
        for e, r, past in rims:
            near = [corners[k][0][e] for k in range(2)]
            middle = parts[e] + weights[e] * field[r, :, cols(c)]
            middle = middle + at_ends(along[0][e] * near[0], along[1][e] * near[1], line)
            second[c, block.along(past), :] = middle
            own_ends, past_ends = [], []
            for k, d, beyond in ends:
                index = (slice(r, r + 1), cols(c))
                outside = arrived(even_d, odd_d, depth_odd, of_deep(rows, c, 0, r, 1))[k]
                next_cell = arrived(even_d, odd_d, depth_odd, of_deep(rows, c, 6, r, 1))[k]
                next_weight = arrived(even_d, odd_d, depth_odd, of_deep(rows, c, 7, e, 1))[k]
                _, far_cell, part, weight = (x[e] for x in corners[k])
                past_ends.append(part + weight * outside)
                own_ends.append(sides[k, 0, *index] + sides[k, 1, *index] * near[k])
                cell(second, c, past, beyond, past_ends[k])
                cell(second, c, r, beyond, own_ends[k])
                cell(second, c, r, 2 * beyond - d, next_cell + next_weight * far_cell)
            own_along = [own_d[6 * e + k : 6 * e + k + 1, cols(c)] for k in range(2)]
            value = partly[e, :, cols(c)] + own_w[e, :, cols(c)] * middle
            value = value + at_ends(
                own_along[0] * own_ends[0], own_along[1] * own_ends[1], line
            )
            third[c, block.along(r), :] = value
            front[e, :, cols(c)] = value
            value = fronts[e] + weights[e] * middles[3 * e, :, cols(c)]
            third[c, block.along(past), :] = value + at_ends(
                along[0][e] * past_ends[0], along[1][e] * past_ends[1], line
            )

    over(len(every), around, 2)
    saves = [
        pltpu.make_async_copy(front.at[e], front_far.at[r], sems.at[e]) for e, r, past in rims
    ]
    for save in saves:
        save.start()
    for k, d, beyond in ends:
        items = [
            [
                arrived(even_d, odd_d, depth_odd, of_deep(rows, c, 2 + i))[k]
                for i in range(4)
            ]
            for c in every
        ]
        values = block.section_slab(second, 0, beyond, rows, lambda c: items[c])
        block.put(third, block.across(0, beyond, rows), values)

    def shine(d, carry):
        shallow, center, deep = (block.slab(third, 0, d + i, rows) for i in (-1, 0, 1))
        before, after = beside(center)
        above, below = block.slab(third, -1, d, rows), block.slab(third, 1, d, rows)
        result = []
        for c in every:
            through, total, red, green = carry[c]
            u = center[c]
            grad_row = below[c] - above[c]
            grad_deep = deep[c] - shallow[c]
            grad_col = after[c] - before[c]
            lighting = 0.48 * grad_row + 0.64 * grad_deep + 0.6 * grad_col
            magnitude = grad_row * grad_row + grad_deep * grad_deep + grad_col * grad_col + 0.4
            shade = 0.35 + 0.65 * lighting * lighting / magnitude
            passed = jnp.exp(-opacity * u)
            weight = through * (1.0 - passed) * shade
            colored = weight * u
            result.append((through * passed, total + weight, red + colored, green + colored * u))
        return tuple(result)

    zero, one = jnp.zeros((rows, lanes), jnp.float32), jnp.ones((rows, lanes), jnp.float32)
    carry = tuple((one, zero, zero, zero) for _ in every)
    carry = lax.fori_loop(0, depth, shine, carry, unroll=8)
    for c, (through, total, red, green) in enumerate(carry):
        partial[0, :, cols(c)] = red
        partial[1, :, cols(c)] = green
        partial[2, :, cols(c)] = total - red
        partial[3, :, cols(c)] = through
    for save in saves:
        save.wait()


def vmem(shape):
    return pltpu.VMEM(shape, jnp.float32)


def here(value):
    return pltpu.with_memory_space_constraint(value, pltpu.VMEM)


def far(value):
    return pltpu.with_memory_space_constraint(value, pltpu.HBM)


def shards(field, diffusivity, velocity):
    rows, depth, width = field.shape
    count = width // lanes
    block = Block(rows, depth, width)
    groups = lax.axis_size("depth")
    params = pltpu.CompilerParams(vmem_limit_bytes=24 * 2**20)
    in_hbm = pl.BlockSpec(memory_space=pltpu.HBM)

    own_types = [pltpu.VMEM(x.shape, x.dtype) for x in (field, diffusivity, velocity)]
    *own, even_d, odd_d, odd_f, near = pl.pallas_call(
        pack_kernel,
        in_specs=[in_hbm] * 3,
        out_shape=own_types
        + [vmem((count * deep_rows(rows), lanes))] * 2
        + [vmem((depth, width)), vmem((2, rows, width))],
        scratch_shapes=[
            vmem((count, rows * (depth + pack_gap), lanes)),
            vmem((4, count, rows * (depth + pack_gap), lanes)),
            pltpu.SemaphoreType.DMA((halves, 5)),
        ],
        compiler_params=params,
        name="pack",
    )(far(field), far(diffusivity), far(velocity))
    odd_f = here(swap_pairs(odd_f, "rows", 1))
    even_d = here(swap_pairs(even_d, "depth", 0))
    odd_d = here(swap_pairs(odd_d, "depth", 1))
    own = [here(x) for x in own]
    spare_rows = (2 * depth + 2 + 7) // 8 * 8
    odd_x, even_x, *kept = pl.pallas_call(
        spare_kernel,
        out_shape=[vmem((spare_rows, width)), vmem((depth + spare_rows + 8, width))]
        + [vmem((4, depth, width)), vmem((2, depth, width)), vmem((8, width))],
        scratch_shapes=[vmem((4, count, depth + 2 * margin, lanes))],
        compiler_params=params,
        cost_estimate=pl.CostEstimate(
            flops=40 * field.size, bytes_accessed=4 * field.size, transcendentals=0
        ),
        name="spare",
    )(*own)
    odd_x = here(swap_pairs(odd_x, "rows", 1))
    even_x = here(swap_pairs(even_x, "rows", 0))
    kept = [here(x) for x in kept]
    odd_2, even_2, middles, partly, sides = pl.pallas_call(
        edge_kernel,
        out_shape=[
            vmem((depth + 8, width)),
            vmem((depth + 8, width)),
            vmem((4, depth, width)),
            vmem((2, depth, width)),
            vmem((2, 2, rows, width)),
        ],
        scratch_shapes=[
            vmem((2, count, depth + 2 * margin, lanes)),
            vmem((count, 8 * (rows + 1), lanes)),
        ],
        compiler_params=params,
        name="edge",
    )(*own[1:], even_d, odd_d, odd_f, even_x, here(near), *kept)
    odd_2 = here(swap_pairs(odd_2, "rows", 1))
    even_2 = here(swap_pairs(even_2, "rows", 0))
    middles, partly, sides = here(middles), here(partly), here(sides)
    held = [vmem((count, (rows + 2) * block.pitch + margin, lanes))] * 2
    held += [pltpu.HBM(field.shape, field.dtype)]
    in_vmem = pl.BlockSpec(memory_space=pltpu.VMEM)
    second, third, front = pl.pallas_call(
        inner_kernel,
        out_shape=held,
        out_specs=[in_vmem] * 2 + [in_hbm],
        scratch_shapes=[
            vmem((count, (rows + 2) * block.pitch + margin, lanes)),
            vmem(field.shape),
            pltpu.SemaphoreType.DMA,
        ],
        compiler_params=params,
        cost_estimate=pl.CostEstimate(
            flops=80 * field.size, bytes_accessed=8 * field.size, transcendentals=0
        ),
        name="inner",
    )(*own, even_d, odd_d, middles, sides)
    opacity = opacity_total / (depth * groups)
    _, _, front, partial = pl.pallas_call(
        lambda *refs: rim_kernel(opacity, *refs),
        in_specs=[in_vmem] * 14 + [in_hbm],
        out_shape=held + [vmem((4, rows, width))],
        out_specs=[in_vmem] * 2 + [in_hbm, in_vmem],
        scratch_shapes=[vmem((2, depth, width)), pltpu.SemaphoreType.DMA((2,))],
        input_output_aliases={12 + i: i for i in range(3)},
        compiler_params=params,
        name="rim",
    )(
        own[0], even_d, odd_d, odd_x, even_x, odd_2, even_2, *kept[1:], middles, partly, sides,
        here(second), here(third), far(front),
    )

    position = lax.axis_index("depth")
    split = partial.reshape(4, rows, groups, width // groups)
    parts = {}
    for apart in range(groups):
        part = lax.dynamic_index_in_dim(split, position ^ apart, 2, keepdims=False)
        if apart:
            part = lax.ppermute(part, "depth", [(i, i ^ apart) for i in range(groups)])
        parts[apart] = part
    parts = jnp.stack([parts[-apart % groups] for apart in range(groups)])
    picture = None
    for s in range(groups):
        apart = position ^ s
        segment = lax.dynamic_index_in_dim(parts, -apart % groups, 0, keepdims=False)
        if picture is None:
            colors, through = segment[:3], segment[3:]
            picture = (colors, through)
        else:
            colors = colors + through * segment[:3]
            through = through * segment[3:]
    return front, jnp.concatenate([colors, through], axis=0)


def solution(mesh):
    return jax.shard_map(
        shards,
        mesh=mesh,
        in_specs=(
            P("rows", "depth", None),
            P("rows", "depth", None),
            P(None, "rows", "depth", None),
        ),
        out_specs=(P("rows", "depth", None), P(None, "rows", "depth")),
        check_vma=False,
    )
```
